512 devices in a mesh: seq: 32 (over x, y), head: 16 (over z, core).
Axes of the slice: x: 4, y: 8, z: 8, core: 2. Of those that a mesh axis runs over, the one named last changes fastest.
Arguments:
- queries: bfloat16 [65536, 4096], P(('seq', 'head')), may hold values from -6 to 6
- keys: bfloat16 [65536, 4096], P(('seq', 'head')), may hold values from -6 to 6
- values: bfloat16 [65536, 4096], P(('seq', 'head')), may hold values from -400 to 400
- log_decay: bfloat16 [65536, 32], P(('seq', 'head')), may hold values from -1 to 0
- cached_state: float32 [32, 128, 128], P('head'), may hold values from -384 to 384
- norm_gain: float32 [32, 128], P('head'), may hold values from 0.25 to 1.75
Outputs:
- attended: bfloat16 [65536, 4096], P(('seq', 'head'))
- final_state: float32 [32, 128, 128], P('head', 'seq')
The draws below stay inside these ranges and needn't reach their ends.
All inputs are finite; a program needn't handle non-finite values.
Results may differ from the reference program's by a relative error of at most 0.0035.
Values may be sent and summed in bfloat16 or wider, within the bound.
A program may use at most 64 MiB of HBM per device.

```python
import math
import jax
import jax.numpy as jnp
from jax import lax

HEAD_TOTAL = 32
HD = 128
BLK = 512
SPAN_TOKENS = 65536


def draw_values(key, part):
    key = jax.random.fold_in(key, 7)
    first, second = jax.random.split(key, 2)
    column_scale = jnp.exp(jax.random.uniform(first, (HEAD_TOTAL * HD,), jnp.float32, 0.0, math.log(10.0)))
    base = jnp.clip(jax.random.normal(second, (SPAN_TOKENS, HEAD_TOTAL * HD), jnp.float32), -4.0, 4.0)
    return (base * column_scale[None, :]).astype(jnp.bfloat16)


def draw_log_decay(key, part):
    key = jax.random.fold_in(key, 11)
    every_key = jax.random.split(key, 7)
    share = 0.5
    fast = jax.random.uniform(every_key[0], (HEAD_TOTAL,), jnp.float32) < share
    fast_rate = -1.0 / jax.random.uniform(every_key[1], (HEAD_TOTAL,), jnp.float32, 30.0, 50.0)
    slow_rate = -jnp.exp(jax.random.uniform(every_key[2], (HEAD_TOTAL,), jnp.float32, math.log(0.1), math.log(0.5))) / SPAN_TOKENS
    base_rate = jnp.where(fast, fast_rate, slow_rate)
    segment_count = (SPAN_TOKENS + 255) // 256
    segment_factor = jnp.exp(jax.random.uniform(every_key[3], (segment_count, HEAD_TOTAL), jnp.float32, math.log(0.5), math.log(2.0)))
    rows = jnp.arange(SPAN_TOKENS) // 256
    segment_rows = segment_factor[rows]
    token_factor = jnp.exp(jax.random.uniform(every_key[4], (SPAN_TOKENS, HEAD_TOTAL), jnp.float32, math.log(0.5), math.log(2.0)))
    stable_decay = base_rate[None, :] * segment_rows * token_factor
    window_offset = jax.random.randint(every_key[5], (2,), 0, SPAN_TOKENS)
    window_rows = jnp.any(jnp.arange(SPAN_TOKENS)[:, None] == window_offset[None, :], axis=1)
    window_length = jax.random.uniform(every_key[6], (SPAN_TOKENS, HEAD_TOTAL), jnp.float32, math.log(0.55), math.log(0.8))
    return (stable_decay + jnp.where(window_rows[:, None], window_length, 0.0)).astype(jnp.bfloat16)


def steps_of(own_key, dims, pieces, smallest, largest):
    level = 1.0
    for dim, parts in pieces:
        heights = jax.random.uniform(jax.random.fold_in(jax.random.fold_in(own_key, 6), dim), (parts,), jnp.float32, smallest / len(pieces), largest / len(pieces))
        level = level * jnp.repeat(jnp.exp(heights), dims[dim] // parts).reshape((-1,) + (1,) * (len(dims) - 1 - dim))
    return level


def noise(rng, dims, scale, bound, pieces=(), kind=jnp.bfloat16):
    loudness = steps_of(rng, dims, pieces, -0.22, 0.18) if pieces else 1.0
    array = jax.random.normal(rng, dims, jnp.float32) * scale * loudness
    return jnp.minimum(jnp.maximum(array, -bound), bound).astype(kind)


def setup_inputs(seed: int = 0) -> dict:
    key_list = jax.random.split(jax.random.key(seed), 7)
    queries = noise(key_list[0], (SPAN_TOKENS, HEAD_TOTAL * HD), 1.0, 6.0, ((0, 512),))
    keys = noise(key_list[1], (SPAN_TOKENS, HEAD_TOTAL * HD), 1.0, 6.0, ((0, 512),))
    values = draw_values(jax.random.fold_in(key_list[6], 71), 0)
    log_decay = draw_log_decay(jax.random.fold_in(key_list[6], 71), 0)
    cached_state = noise(key_list[4], (HEAD_TOTAL, HD, HD), 64.0, 384.0, ((0, 16),), jnp.float32)
    norm_gain = jnp.clip(1.0 + 0.15 * jax.random.normal(key_list[5], (HEAD_TOTAL, HD), jnp.float32), 0.25, 1.75)
    return dict(queries=queries, keys=keys, values=values, log_decay=log_decay, cached_state=cached_state, norm_gain=norm_gain)


def reference(queries, keys, values, log_decay, cached_state, norm_gain):
    block_count = SPAN_TOKENS // BLK
    query_blocks = queries.reshape(block_count, BLK, HEAD_TOTAL, HD)
    key_blocks = keys.reshape(block_count, BLK, HEAD_TOTAL, HD)
    value_blocks = values.reshape(block_count, BLK, HEAD_TOTAL, HD)
    decay_blocks = log_decay.astype(jnp.float32).reshape(block_count, BLK, HEAD_TOTAL)
    positions = jnp.arange(BLK, dtype=jnp.int32)
    lower_mask = positions[:, None] >= positions[None, :]

    def advance(state_now, block):
        query_rows, key_rows, value_rows, log_rows = block
        running = jnp.cumsum(log_rows, axis=0)
        query_wide = query_rows.astype(jnp.float32)
        key_wide = key_rows.astype(jnp.float32)
        value_wide = value_rows.astype(jnp.float32)
        scores = jnp.einsum('thd,shd->hts', query_wide, key_wide)
        across = running.T
        log_gaps = across[:, :, None] - across[:, None, :]
        decay_mask = jnp.where(lower_mask[None], jnp.exp(jnp.where(lower_mask[None], log_gaps, 0.0)), 0.0)
        weights = lax.optimization_barrier((scores * decay_mask).astype(jnp.bfloat16)).astype(jnp.float32)
        within = jnp.einsum('hts,shd->thd', weights, value_wide)
        carried = jnp.einsum('thd,hde->the', query_wide, state_now, precision=lax.Precision.HIGHEST)
        carried = carried * jnp.exp(running)[:, :, None]
        ending = running[-1]
        keys_scaled = key_wide * jnp.exp(ending[None, :] - running)[:, :, None]
        added = jnp.einsum('thd,the->hde', keys_scaled, value_wide, precision=lax.Precision.HIGHEST)
        state_next = jnp.exp(ending)[:, None, None] * state_now + added
        return (state_next, within + carried)
    final_state, mixed = lax.scan(advance, cached_state, (query_blocks, key_blocks, value_blocks, decay_blocks))
    mixed = mixed.reshape(SPAN_TOKENS, HEAD_TOTAL, HD)
    scale_rows = lax.rsqrt(lax.optimization_barrier(jnp.mean(mixed * mixed, axis=-1, keepdims=True)) + 1e-06)
    normed = mixed * scale_rows * norm_gain[None]
    return (normed.astype(jnp.bfloat16).reshape(SPAN_TOKENS, HEAD_TOTAL * HD), final_state)
```

```python
import functools

import jax
import jax.numpy as jnp
from jax import lax
from jax.experimental import pallas as pl
from jax.experimental.pallas import tpu as pltpu
from jax.sharding import PartitionSpec as P

HD = 128
ROWS = 128
SPAN = 2 * ROWS
PAIR = 2 * HD
MSG = PAIR + 16
PIECE = 8
F32 = jnp.float32
BF16 = jnp.bfloat16
NEVER = -1e30


def dot(a, b, dims=((1,), (0,))):
    return lax.dot_general(a, b, (dims, ((), ())), preferred_element_type=F32)


def three(x):
    first = x.astype(BF16)
    rest = x - first.astype(F32)
    second = rest.astype(BF16)
    third = (rest - second.astype(F32)).astype(BF16)
    return first.astype(F32), second.astype(F32), third.astype(F32)


def tile_of(rows):
    at = lax.broadcasted_iota(jnp.int32, (16, HD), 0)
    tile = jnp.zeros((16, HD), F32)
    for u, row in enumerate(rows):
        for part, value in enumerate(three(row)):
            tile = jnp.where(at == 8 * u + part, value, tile)
    return tile.astype(BF16)


def row_of(tile, u):
    wide = tile.astype(F32)
    return wide[8 * u : 8 * u + 1] + wide[8 * u + 1 : 8 * u + 2] + wide[8 * u + 2 : 8 * u + 3]


def kernel(
    ns, nz,
    q_ref, k_ref, v_ref, ld_ref, cached_ref, gain_ref,
    att_ref, fin_ref,
    qkv, ld_all, lower, run_all, within,
    l_send, l_recv, x_send, x_recv, e_send, e_recv, s_send, s_recv, out,
    own_sem, in_send, in_recv, ld_sem, l_ss, l_rs, x_ss, x_rs, e_ss, e_rs, s_ss, s_rs, o_own, o_ss, o_rs,
):
    seq = lax.axis_index("seq")
    head = lax.axis_index("head")
    z = lax.div(head, 2)
    core = lax.rem(head, 2)
    other = 1 - core
    partner = 2 * z + other
    mine_rows = pl.ds(pl.multiple_of(core * ROWS, ROWS), ROWS)
    other_rows = pl.ds(pl.multiple_of(other * ROWS, ROWS), ROWS)
    sources = (k_ref, v_ref, q_ref)

    def columns(block, which):
        return pl.ds(pl.multiple_of((2 * block + which) * PAIR, PAIR), PAIR)

    def order(t):
        return lax.rem(z + 1 + t, nz)

    def own_copy(a, b):
        return pltpu.make_async_copy(
            sources[a].at[:, columns(b, core)], qkv.at[a, b, mine_rows], own_sem.at[a, b]
        )

    def swap_copy(a, b):
        return pltpu.make_async_remote_copy(
            sources[a].at[:, columns(b, other)], qkv.at[a, b, mine_rows],
            in_send.at[a, b], in_recv.at[a, b],
            device_id=(seq, partner), device_id_type=pl.DeviceIdType.MESH,
        )

    def swap_arrival(a, b):
        return pltpu.make_async_remote_copy(
            sources[a].at[:, columns(b, other)], qkv.at[a, b, other_rows],
            in_send.at[a, b], in_recv.at[a, b],
            device_id=(seq, partner), device_id_type=pl.DeviceIdType.MESH,
        )

    ld_copy = pltpu.make_async_remote_copy(
        ld_all.at[mine_rows], ld_all.at[mine_rows], ld_sem.at[0], ld_sem.at[1],
        device_id=(seq, partner), device_id_type=pl.DeviceIdType.MESH,
    )
    ld_arrival = pltpu.make_async_remote_copy(
        ld_all.at[other_rows], ld_all.at[other_rows], ld_sem.at[0], ld_sem.at[1],
        device_id=(seq, partner), device_id_type=pl.DeviceIdType.MESH,
    )

    def over_z(src, dst, ss, rs, to, slot):
        return pltpu.make_async_remote_copy(
            src.at[to], dst.at[slot], ss.at[to], rs.at[slot],
            device_id=(seq, 2 * to + core), device_id_type=pl.DeviceIdType.MESH,
        )

    def over_seq(src, dst, ss, rs, to, slot):
        return pltpu.make_async_remote_copy(
            src.at[to], dst.at[slot], ss.at[to], rs.at[slot],
            device_id=(to, head), device_id_type=pl.DeviceIdType.MESH,
        )

    barrier = pltpu.get_barrier_semaphore()
    pl.semaphore_signal(barrier, inc=1, device_id=(seq, partner), device_id_type=pl.DeviceIdType.MESH)

    @pl.loop(1, nz)
    def _(t):
        pl.semaphore_signal(
            barrier, inc=1, device_id=(seq, 2 * lax.rem(z + t, nz) + core), device_id_type=pl.DeviceIdType.MESH
        )

    @pl.loop(1, ns)
    def _(t):
        pl.semaphore_signal(
            barrier, inc=1, device_id=(lax.rem(seq + t, ns), head), device_id_type=pl.DeviceIdType.MESH
        )

    for a in range(3):
        @pl.loop(0, nz)
        def _(t):
            own_copy(a, order(t)).start()

    wide = dot(
        ld_ref[...],
        (lax.broadcasted_iota(jnp.int32, (ld_ref.shape[1], HD), 0)
         == lax.broadcasted_iota(jnp.int32, (ld_ref.shape[1], HD), 1)).astype(F32).astype(BF16),
    )
    ld_all[mine_rows, :] = wide.astype(BF16)
    causal = lax.broadcasted_iota(jnp.int32, (SPAN, SPAN), 0) >= lax.broadcasted_iota(jnp.int32, (SPAN, SPAN), 1)
    lower[...] = causal.astype(F32).astype(BF16)

    pl.semaphore_wait(barrier, 1 + (nz - 1) + (ns - 1))

    ld_copy.start()
    for a in range(3):
        @pl.loop(0, nz)
        def _(t):
            swap_copy(a, order(t)).start()

    ld_copy.wait_send()
    ld_arrival.wait_recv()

    @pl.loop(0, nz)
    def _(t):
        b = order(t)
        for a in range(2):
            own_copy(a, b).wait()
            swap_arrival(a, b).wait_recv()
        ends = []
        for u in range(2):
            which = 4 * b + 2 * core + u
            pick = (lax.broadcasted_iota(jnp.int32, (HD, HD), 0) == which).astype(F32).astype(BF16)
            token = dot(ld_all[...], pick).astype(BF16)
            run = dot(lower[...], token)
            run_all[2 * b + u] = run
            end = run[SPAN - 1 : SPAN]
            ends.append(end)
            keys = qkv[0, b, :, u * HD : (u + 1) * HD].astype(F32)
            scaled = keys * jnp.exp(end - run)
            high = scaled.astype(BF16)
            low = (scaled - high.astype(F32)).astype(BF16)
            both = dot(
                jnp.concatenate([high, low], axis=1), qkv[1, b, :, u * HD : (u + 1) * HD], ((0,), (0,))
            )
            l_send[b, u * HD : (u + 1) * HD, :] = (both[:HD] + both[HD:]).astype(BF16)
        l_send[b, PAIR:MSG, :] = tile_of(ends)

        @pl.when(t < nz - 1)
        def _():
            over_z(l_send, l_recv, l_ss, l_rs, b, z).start()

    l_recv[z] = l_send[z]

    def inside(b):
        own_copy(2, b).wait()
        swap_arrival(2, b).wait_recv()
        for u in range(2):
            which = 4 * b + 2 * core + u
            pick = (lax.broadcasted_iota(jnp.int32, (8, HD), 1) == which).astype(F32).astype(BF16)
            token = dot(pick, ld_all[...], ((1,), (1,))).astype(BF16)
            across = dot(token, lower[...], ((1,), (1,)))[:1]
            run = run_all[2 * b + u]
            keys = qkv[0, b, :, u * HD : (u + 1) * HD]
            queries = qkv[2, b, :, u * HD : (u + 1) * HD]
            values = qkv[1, b, :, u * HD : (u + 1) * HD]
            scores = dot(queries, keys, ((1,), (1,)))
            gap = jnp.concatenate([run, run], axis=1) - across
            here = (
                lax.broadcasted_iota(jnp.int32, (SPAN, SPAN), 0)
                >= lax.broadcasted_iota(jnp.int32, (SPAN, SPAN), 1)
            )
            weights = (scores * jnp.exp(jnp.where(here, gap, NEVER))).astype(BF16)
            within[2 * b + u] = dot(weights, values)

    @pl.loop(0, nz)
    def _(t):
        inside(t)

    first4 = lax.broadcasted_iota(jnp.int32, (8, HD), 0) < 4

    def add(b, sums):
        @pl.when(b != z)
        def _():
            over_z(l_send, l_recv, l_ss, l_rs, b, b).wait_recv()

        tile = l_recv[b, PAIR:MSG, :]
        after = []
        for u in range(2):
            decay, state = sums[2 * u], sums[2 * u + 1]
            step = row_of(tile, u)
            after += [decay + step, jnp.exp(step) * state + l_recv[b, u * HD : (u + 1) * HD, :].astype(F32)]
        return tuple(after)

    none = (jnp.zeros((1, HD), F32), jnp.zeros((HD, HD), F32)) * 2
    decay0, state0, decay1, state1 = lax.fori_loop(0, nz, add, none)
    decays = jnp.where(first4, decay0, decay1)
    for g in range(ns // 2):
        top, bottom = state0[8 * g : 8 * g + 8], state1[8 * g : 8 * g + 8]
        x_send[2 * g, 0:8, :] = jnp.where(first4, top, pltpu.roll(bottom, 4, 0))
        x_send[2 * g + 1, 0:8, :] = jnp.where(first4, pltpu.roll(top, 4, 0), bottom)
        x_send[2 * g, 8:16, :] = decays
        x_send[2 * g + 1, 8:16, :] = decays

    @pl.loop(1, ns)
    def _(t):
        over_seq(x_send, x_recv, x_ss, x_rs, lax.rem(seq + t, ns), seq).start()

    x_recv[seq] = x_send[seq]

    at = pl.ds(pl.multiple_of(lax.div(seq, 2) * 8, 8), 8)
    top, bottom = cached_ref[0, at, :], cached_ref[1, at, :]
    even = jnp.where(first4, top, pltpu.roll(bottom, 4, 0))
    odd = jnp.where(first4, pltpu.roll(top, 4, 0), bottom)
    start = jnp.where(lax.rem(seq, 2) == 0, even, odd)

    def through(i, piece):
        @pl.when(i != seq)
        def _():
            over_seq(x_send, x_recv, x_ss, x_rs, i, i).wait_recv()

        e_send[i] = piece

        @pl.when(i != seq)
        def _():
            over_seq(e_send, e_recv, e_ss, e_rs, i, seq).start()

        return jnp.exp(x_recv[i, 8:16, :]) * piece + x_recv[i, 0:8, :]

    last = lax.fori_loop(0, ns, through, start)
    fin_ref[0] = last[0:4]
    fin_ref[1] = last[4:8]
    e_recv[seq] = e_send[seq]

    @pl.loop(1, ns)
    def _(t):
        over_seq(e_send, e_recv, e_ss, e_rs, lax.rem(seq + t, ns), lax.rem(seq + t, ns)).wait_recv()

    tops, bottoms = [], []
    for g in range(ns // 2):
        even, odd = e_recv[2 * g], e_recv[2 * g + 1]
        tops.append(jnp.where(first4, even, pltpu.roll(odd, 4, 0)))
        bottoms.append(jnp.where(first4, pltpu.roll(even, 4, 0), odd))
    entry = (jnp.concatenate(tops, axis=0), jnp.concatenate(bottoms, axis=0))
    gains = tile_of([gain_ref[0:1, :], gain_ref[1:2, :]])

    def give(b, states):
        tile = l_recv[b, PAIR:MSG, :]
        after = []
        for u in range(2):
            s_send[b, u * HD : (u + 1) * HD, :] = states[u].astype(BF16)
            after.append(
                jnp.exp(row_of(tile, u)) * states[u] + l_recv[b, u * HD : (u + 1) * HD, :].astype(F32)
            )
        s_send[b, PAIR:MSG, :] = gains

        @pl.when(b != z)
        def _():
            over_z(s_send, s_recv, s_ss, s_rs, b, z).start()

        return tuple(after)

    lax.fori_loop(0, nz, give, entry)
    s_recv[z] = s_send[z]

    def out_own(b):
        return pltpu.make_async_copy(out.at[b, mine_rows], att_ref.at[:, columns(b, core)], o_own.at[b])

    def out_swap(b):
        return pltpu.make_async_remote_copy(
            out.at[b, other_rows], att_ref.at[:, columns(b, core)], o_ss.at[b], o_rs.at[b],
            device_id=(seq, partner), device_id_type=pl.DeviceIdType.MESH,
        )

    def out_arrival(b):
        return pltpu.make_async_remote_copy(
            out.at[b, other_rows], att_ref.at[:, columns(b, other)], o_ss.at[b], o_rs.at[b],
            device_id=(seq, partner), device_id_type=pl.DeviceIdType.MESH,
        )

    @pl.loop(0, nz)
    def _(t):
        b = lax.rem(z + t, nz)

        @pl.when(t > 0)
        def _():
            over_z(s_send, s_recv, s_ss, s_rs, b, b).wait_recv()

        tile = s_recv[b, PAIR:MSG, :]
        for u in range(2):
            queries = qkv[2, b, :, u * HD : (u + 1) * HD]
            carried = dot(queries, s_recv[b, u * HD : (u + 1) * HD, :])
            mixed = within[2 * b + u] + carried * jnp.exp(run_all[2 * b + u])
            mean = jnp.mean(mixed * mixed, axis=1, keepdims=True)
            normed = mixed * lax.rsqrt(mean + 1e-6) * row_of(tile, u)
            out[b, :, u * HD : (u + 1) * HD] = normed.astype(BF16)
        out_own(b).start()
        out_swap(b).start()

    for a in range(3):
        @pl.loop(0, nz)
        def _(t):
            swap_copy(a, t).wait_send()

    @pl.loop(1, nz)
    def _(t):
        b = lax.rem(z + t, nz)
        over_z(l_send, l_recv, l_ss, l_rs, b, z).wait_send()
        over_z(s_send, s_recv, s_ss, s_rs, b, z).wait_send()

    @pl.loop(1, ns)
    def _(t):
        i = lax.rem(seq + t, ns)
        over_seq(x_send, x_recv, x_ss, x_rs, i, seq).wait_send()
        over_seq(e_send, e_recv, e_ss, e_rs, i, seq).wait_send()

    @pl.loop(0, nz)
    def _(b):
        out_own(b).wait()
        out_swap(b).wait_send()
        out_arrival(b).wait_recv()


def local(ns, nz, queries, keys, values, log_decay, cached_state, norm_gain):
    anywhere = pl.BlockSpec(memory_space=pl.ANY)
    vmem = pl.BlockSpec(memory_space=pltpu.VMEM)
    dma = pltpu.SemaphoreType.DMA
    return pl.pallas_call(
        functools.partial(kernel, ns, nz),
        out_shape=(
            jax.ShapeDtypeStruct(queries.shape, BF16),
            jax.ShapeDtypeStruct((2, HD // ns, HD), F32),
        ),
        in_specs=[anywhere, anywhere, anywhere, vmem, vmem, vmem],
        out_specs=(anywhere, vmem),
        scratch_shapes=[
            pltpu.VMEM((3, nz, SPAN, PAIR), BF16),
            pltpu.VMEM((SPAN, HD), BF16),
            pltpu.VMEM((SPAN, SPAN), BF16),
            pltpu.VMEM((2 * nz, SPAN, HD), F32),
            pltpu.VMEM((2 * nz, SPAN, HD), F32),
            pltpu.VMEM((nz, MSG, HD), BF16),
            pltpu.VMEM((nz, MSG, HD), BF16),
            pltpu.VMEM((ns, 16, HD), F32),
            pltpu.VMEM((ns, 16, HD), F32),
            pltpu.VMEM((ns, PIECE, HD), F32),
            pltpu.VMEM((ns, PIECE, HD), F32),
            pltpu.VMEM((nz, MSG, HD), BF16),
            pltpu.VMEM((nz, MSG, HD), BF16),
            pltpu.VMEM((nz, SPAN, PAIR), BF16),
            dma((3, nz)), dma((3, nz)), dma((3, nz)), dma((2,)),
            dma((nz,)), dma((nz,)), dma((ns,)), dma((ns,)), dma((ns,)), dma((ns,)),
            dma((nz,)), dma((nz,)), dma((nz,)), dma((nz,)), dma((nz,)),
        ],
        compiler_params=pltpu.CompilerParams(
            collective_id=0, has_side_effects=True, vmem_limit_bytes=60 * 1024 * 1024
        ),
        cost_estimate=pl.CostEstimate(flops=10**9, bytes_accessed=8 * 2**20, transcendentals=2 * 10**6),
    )(queries, keys, values, log_decay, cached_state, norm_gain)


def solution(mesh):
    rows = P(("seq", "head"), None)
    return jax.shard_map(
        functools.partial(local, mesh.shape["seq"], mesh.shape["head"] // 2),
        mesh=mesh,
        in_specs=(rows, rows, rows, rows, P("head", None, None), P("head", None)),
        out_specs=(rows, P("head", "seq", None)),
        check_vma=False,
    )
```

```python
import functools

import jax
import jax.numpy as jnp
from jax import lax
from jax.experimental import pallas as pl
from jax.experimental.pallas import tpu as pltpu
from jax.sharding import PartitionSpec as P

HD = 128
ROWS = 128
SPAN = 2 * ROWS
PAIR = 2 * HD
HALF = HD // 2
PIECE = 8
F32 = jnp.float32
BF16 = jnp.bfloat16
NEVER = -1e30
MESH = pl.DeviceIdType.MESH


def dot(a, b, dims=((1,), (0,))):
    return lax.dot_general(a, b, (dims, ((), ())), preferred_element_type=F32)


def kernel(
    ns, nz,
    q_ref, k_ref, v_ref, ld_ref, cached_ref, gain_ref,
    att_ref, fin_ref,
    tokens, ld_all, decay_rows, run_rows, fade_rows, end_rows, lower, run_all, within,
    l_send, l_recv, x_send, x_recv, e_send, e_recv, s_send, s_recv, out, fin_all, cached, gain, z_send, z_recv, d_send, d_recv,
    own_sem, in_send, in_recv, ld_sem, l_ss, l_rs, x_ss, x_rs, e_ss, e_rs, s_ss, s_rs, o_own, o_ss, o_rs, f_sem, small_sem,
    z_ss, z_rs, d_ss, d_rs,
):
    seq = lax.axis_index("seq")
    head = lax.axis_index("head")
    z = lax.div(head, 2)
    core = lax.rem(head, 2)
    other = 1 - core
    partner = 2 * z + other
    group = lax.div(seq, 2)
    turn = lax.rem(seq, 2)
    sources = (k_ref, v_ref, q_ref)

    def columns(block, which):
        return pl.ds(pl.multiple_of((2 * block + which) * PAIR, PAIR), PAIR)

    def head_columns(block, u):
        return pl.ds(pl.multiple_of((2 * block + core) * PAIR + u * HD, HD), HD)

    def rows_of(a, block, u):
        at = head_columns(block, u)
        return jnp.concatenate([tokens[a, 0, :, at], tokens[a, 1, :, at]], axis=0)

    def near(t):
        step = lax.div(t + 1, 2)
        return lax.rem(z + jnp.where(lax.rem(t, 2) == 1, step, nz - step), nz)

    def order(t):
        return near(nz - 1 - t)

    def own_copy(a):
        return pltpu.make_async_copy(sources[a], tokens.at[a, core], own_sem.at[a])

    def to_partner(src, dst, ss, rs):
        return pltpu.make_async_remote_copy(
            src, dst, ss, rs, device_id=(seq, partner), device_id_type=MESH
        )

    def swap_copy(a, b):
        at = columns(b, other)
        return to_partner(sources[a].at[:, at], tokens.at[a, core, :, at], in_send.at[a, b], in_recv.at[a, b])

    def swap_arrival(a, b):
        at = columns(b, core)
        return to_partner(sources[a].at[:, at], tokens.at[a, other, :, at], in_send.at[a, b], in_recv.at[a, b])

    ld_copy = to_partner(ld_all.at[core], ld_all.at[core], ld_sem.at[0], ld_sem.at[1])
    ld_arrival = to_partner(ld_all.at[other], ld_all.at[other], ld_sem.at[0], ld_sem.at[1])

    part_rows = (pl.ds(0, HALF), pl.ds(HALF, HALF))
    near_ns = ns // 4

    def over_z(src, dst, ss, rs, u, part, to, slot):
        return pltpu.make_async_remote_copy(
            src.at[u, to, part_rows[part]], dst.at[u, slot, part_rows[part]],
            ss.at[u, part, to], rs.at[u, part, slot],
            device_id=(seq, 2 * to + core), device_id_type=MESH,
        )

    def facts_copy(to, slot):
        return pltpu.make_async_remote_copy(
            z_send.at[to], z_recv.at[slot], z_ss.at[to], z_rs.at[slot],
            device_id=(seq, 2 * to + core), device_id_type=MESH,
        )

    def decay_copy(to, slot):
        return pltpu.make_async_remote_copy(
            d_send.at[lax.rem(to, 2)], d_recv.at[slot], d_ss.at[to], d_rs.at[slot],
            device_id=(to, head), device_id_type=MESH,
        )

    def piece_rows(g):
        return pl.ds(pl.multiple_of(g * PIECE, PIECE), PIECE)

    def sum_copy(u, g, slot):
        return pltpu.make_async_remote_copy(
            x_send.at[u, g], x_recv.at[slot], x_ss.at[u, g], x_rs.at[slot],
            device_id=(2 * g + u, head), device_id_type=MESH,
        )

    def entry_copy(u, g, to):
        return pltpu.make_async_remote_copy(
            e_send.at[to], e_recv.at[u, piece_rows(g)], e_ss.at[to], e_rs.at[u, g],
            device_id=(to, head), device_id_type=MESH,
        )

    barrier = pltpu.get_barrier_semaphore()
    pl.semaphore_signal(barrier, inc=1, device_id=(seq, partner), device_id_type=MESH)

    @pl.loop(1, nz)
    def _(t):
        pl.semaphore_signal(
            barrier, inc=1, device_id=(seq, 2 * lax.rem(z + t, nz) + core), device_id_type=MESH
        )

    @pl.loop(1, ns)
    def _(t):
        pl.semaphore_signal(barrier, inc=1, device_id=(lax.rem(seq + t, ns), head), device_id_type=MESH)

    ld_own = pltpu.make_async_copy(ld_ref, ld_all.at[core], small_sem.at[0])
    cached_own = pltpu.make_async_copy(cached_ref.at[turn, piece_rows(group)], cached, small_sem.at[1])
    gain_own = pltpu.make_async_copy(gain_ref, gain, small_sem.at[2])
    ld_own.start()
    for a in range(3):
        own_copy(a).start()
    cached_own.start()
    gain_own.start()
    causal = lax.broadcasted_iota(jnp.int32, (SPAN, SPAN), 0) >= lax.broadcasted_iota(jnp.int32, (SPAN, SPAN), 1)
    lower[...] = causal.astype(F32).astype(BF16)

    ld_own.wait()
    pl.semaphore_wait(barrier, 1 + (nz - 1) + (ns - 1))

    ld_copy.start()

    @pl.loop(0, nz)
    def _(t):
        for a in range(2):
            swap_copy(a, order(t)).start()

    def swaps_done():
        ld_copy.wait_send()

        @pl.loop(0, nz)
        def _(t):
            for a in range(3):
                swap_copy(a, t).wait_send()

    ld_arrival.wait_recv()
    for half in range(2):
        decay_rows[:, half * ROWS : (half + 1) * ROWS] = ld_all[half].astype(F32)
    run = dot(decay_rows[...].astype(BF16), lower[...], ((1,), (1,)))
    run_rows[...] = run
    fade_rows[...] = jnp.exp(run[:, SPAN - 1 : SPAN] - run)
    end_rows[...] = jnp.broadcast_to(run[:, SPAN - 1 : SPAN], end_rows.shape)
    gain_own.wait()

    @pl.loop(0, nz)
    def _(t):
        b = order(t)
        first = 4 * b + 2 * core
        at = lax.broadcasted_iota(jnp.int32, (8, HD), 0)
        tile = jnp.where(at == 0, end_rows[pl.ds(first, 1), :], end_rows[pl.ds(first + 1, 1), :])
        z_send[b] = jnp.where(at < 2, tile, jnp.where(at == 2, gain[0:1, :], gain[1:2, :]))

        @pl.when(t < nz - 1)
        def _():
            facts_copy(b, z).start()

    z_recv[z] = z_send[z]
    for a in range(2):
        own_copy(a).wait()

    def send_part(u, part):
        @pl.loop(0, nz - 1)
        def _(t):
            over_z(l_send, l_recv, l_ss, l_rs, u, part, order(t), z).start()

    for u in range(2):
        @pl.loop(0, nz)
        def _(t):
            b = order(t)
            if u == 0:
                for a in range(2):
                    swap_arrival(a, b).wait_recv()
            which = pl.ds(4 * b + 2 * core + u, 1)
            scaled = rows_of(0, b, u).T.astype(F32) * fade_rows[which, :]
            high = scaled.astype(BF16)
            low = (scaled - high.astype(F32)).astype(BF16)
            both = dot(jnp.concatenate([high, low], axis=0), rows_of(1, b, u))
            state = (both[:HD] + both[HD:]).astype(BF16)
            l_send[u, b] = state

            @pl.when(t < nz - 1)
            def _():
                over_z(l_send, l_recv, l_ss, l_rs, u, 0, b, z).start()

        send_part(u, 1)
        l_recv[u, z] = l_send[u, z]
        if u == 0:
            @pl.loop(0, nz)
            def _(t):
                swap_copy(2, t).start()

            @pl.loop(1, nz)
            def _(t):
                facts_copy(lax.rem(z + t, nz), lax.rem(z + t, nz)).wait_recv()

            total = lax.fori_loop(0, nz, lambda b, sums: sums + z_recv[b], jnp.zeros((8, HD), F32))
            for v in range(2):
                d_send[v] = jnp.broadcast_to(total[v : v + 1], (PIECE, HD))

            @pl.loop(1, ns)
            def _(t):
                decay_copy(lax.rem(seq + t, ns), seq).start()

            d_recv[seq] = d_send[turn]

    def l_done():
        @pl.loop(1, nz)
        def _(t):
            for u in range(2):
                for part in range(2):
                    over_z(l_send, l_recv, l_ss, l_rs, u, part, lax.rem(z + t, nz), z).wait_send()

    own_copy(2).wait()

    def inside(b):
        swap_arrival(2, b).wait_recv()
        for u in range(2):
            which = pl.ds(4 * b + 2 * core + u, 1)
            token = jnp.broadcast_to(decay_rows[which, :], (HD, SPAN)).astype(BF16)
            run = dot(lower[...], token, ((1,), (1,)))
            run_all[2 * b + u] = run
            scores = dot(rows_of(2, b, u), rows_of(0, b, u), ((1,), (1,)))
            gap = jnp.concatenate([run, run], axis=1) - run_rows[which, :]
            here = (
                lax.broadcasted_iota(jnp.int32, (SPAN, SPAN), 0)
                >= lax.broadcasted_iota(jnp.int32, (SPAN, SPAN), 1)
            )
            weights = (scores * jnp.exp(jnp.where(here, gap, NEVER))).astype(BF16)
            within[2 * b + u] = dot(weights, rows_of(1, b, u))

    pl.loop(0, nz // 2)(inside)

    def column_sum(u, part):
        def add(b, sums):
            @pl.when(b != z)
            def _():
                over_z(l_send, l_recv, l_ss, l_rs, u, part, b, b).wait_recv()

            return jnp.exp(z_recv[b, u : u + 1, :]) * sums + l_recv[u, b, part_rows[part], :].astype(F32)

        state = lax.fori_loop(0, nz, add, jnp.zeros((HALF, HD), F32))
        for g in range(near_ns):
            x_send[u, near_ns * part + g] = state[PIECE * g : PIECE * (g + 1)]

        @pl.loop(0, near_ns)
        def _(t):
            g = near_ns * part + lax.rem(group + 1 + t, near_ns)

            @pl.when(2 * g + u != seq)
            def _():
                sum_copy(u, g, seq).start()

        @pl.when((turn == u) & (lax.div(group, near_ns) == part))
        def _():
            x_recv[seq] = x_send[u, group]

    def columns_scan(u, part):
        @pl.when((turn == u) & (lax.div(group, near_ns) == part))
        def _():
            @pl.loop(1, ns)
            def _(t):
                sum_copy(u, group, lax.rem(seq + t, ns)).wait_recv()

            piece = cached[...]
            for i in range(ns):
                e_send[i] = piece
                piece = jnp.exp(d_recv[i]) * piece + x_recv[i]
            fin_all[u] = piece

            @pl.loop(0, ns)
            def _(t):
                i = lax.rem(seq + t + 3 * ns // 8, ns)

                @pl.when(i != seq)
                def _():
                    entry_copy(u, group, i).start()

            e_recv[u, piece_rows(group), :] = e_send[seq]

    def give(u, part):
        @pl.loop(near_ns * part, near_ns * (part + 1))
        def _(g):
            @pl.when(2 * g + u != seq)
            def _():
                entry_copy(u, g, seq).wait_recv()

        def step(b, state):
            s_send[u, b, part_rows[part], :] = state.astype(BF16)
            return jnp.exp(z_recv[b, u : u + 1, :]) * state + l_recv[u, b, part_rows[part], :].astype(F32)

        lax.fori_loop(0, nz, step, e_recv[u, HALF * part : HALF * (part + 1), :])

        @pl.loop(0, nz - 1)
        def _(t):
            over_z(s_send, s_recv, s_ss, s_rs, u, part, order(t), z).start()

        if part == 1:
            s_recv[u, z] = s_send[u, z]

    column_sum(0, 0)
    column_sum(0, 1)
    pl.loop(nz // 2, nz)(inside)
    cached_own.wait()

    @pl.loop(1, ns)
    def _(t):
        decay_copy(lax.rem(seq + t, ns), lax.rem(seq + t, ns)).wait_recv()

    columns_scan(0, 0)
    column_sum(1, 0)
    columns_scan(0, 1)
    column_sum(1, 1)
    give(0, 0)
    columns_scan(1, 0)
    give(0, 1)
    columns_scan(1, 1)
    give(1, 0)
    swaps_done()
    l_done()
    give(1, 1)

    def scan_done():
        @pl.loop(0, ns // 2)
        def _(g):
            for u in range(2):
                @pl.when(2 * g + u != seq)
                def _():
                    sum_copy(u, g, seq).wait_send()

        @pl.loop(1, ns)
        def _(t):
            i = lax.rem(seq + t, ns)
            decay_copy(i, seq).wait_send()
            entry_copy(0, group, i).wait_send()

        @pl.loop(1, nz)
        def _(t):
            facts_copy(lax.rem(z + t, nz), z).wait_send()

    def s_done():
        @pl.loop(1, nz)
        def _(t):
            for u in range(2):
                for part in range(2):
                    over_z(s_send, s_recv, s_ss, s_rs, u, part, lax.rem(z + t, nz), z).wait_send()

    def fin_copy(slot):
        return pltpu.make_async_remote_copy(
            fin_all.at[slot], fin_all.at[slot], f_sem.at[0], f_sem.at[1],
            device_id=(2 * group + 1 - turn, head), device_id_type=MESH,
        )

    fin_copy(turn).start()

    mine_rows = pl.ds(pl.multiple_of(core * ROWS, ROWS), ROWS)
    other_rows = pl.ds(pl.multiple_of(other * ROWS, ROWS), ROWS)

    def out_own(b):
        return pltpu.make_async_copy(out.at[b, mine_rows], att_ref.at[:, columns(b, core)], o_own.at[b])

    def out_swap(b):
        return to_partner(out.at[b, other_rows], att_ref.at[:, columns(b, core)], o_ss.at[b], o_rs.at[b])

    def out_arrival(b):
        return to_partner(out.at[b, other_rows], att_ref.at[:, columns(b, other)], o_ss.at[b], o_rs.at[b])

    def output(u):
        @pl.loop(0, nz)
        def _(t):
            b = near(t)

            @pl.when(t > 0)
            def _():
                for part in range(2):
                    over_z(s_send, s_recv, s_ss, s_rs, u, part, b, b).wait_recv()

            carried = dot(rows_of(2, b, u), s_recv[u, b])
            mixed = within[2 * b + u] + carried * jnp.exp(run_all[2 * b + u])
            mean = jnp.mean(mixed * mixed, axis=1, keepdims=True)
            normed = mixed * lax.rsqrt(mean + 1e-6) * z_recv[b, 2 + u : 3 + u, :]
            out[b, :, u * HD : (u + 1) * HD] = normed.astype(BF16)
            if u == 1:
                out_own(b).start()
                out_swap(b).start()

    output(0)
    scan_done()
    output(1)
    fin_copy(1 - turn).wait_recv()
    for u in range(2):
        fin_ref[u] = jnp.where(turn == 0, fin_all[u, 0:4, :], fin_all[u, 4:8, :])

    fin_copy(turn).wait_send()
    s_done()

    @pl.loop(0, nz)
    def _(b):
        out_own(b).wait()
        out_swap(b).wait_send()
        out_arrival(b).wait_recv()


def local(ns, nz, queries, keys, values, log_decay, cached_state, norm_gain):
    anywhere = pl.BlockSpec(memory_space=pl.ANY)
    vmem = pl.BlockSpec(memory_space=pltpu.VMEM)
    dma = pltpu.SemaphoreType.DMA
    heads = log_decay.shape[1]
    return pl.pallas_call(
        functools.partial(kernel, ns, nz),
        out_shape=(
            jax.ShapeDtypeStruct(queries.shape, BF16),
            jax.ShapeDtypeStruct((2, HD // ns, HD), F32),
        ),
        in_specs=[anywhere] * 6,
        out_specs=(anywhere, vmem),
        scratch_shapes=[
            pltpu.VMEM((3, 2) + queries.shape, BF16),
            pltpu.VMEM((2, heads, ROWS), BF16),
            pltpu.VMEM((heads, SPAN), F32),
            pltpu.VMEM((heads, SPAN), F32),
            pltpu.VMEM((heads, SPAN), F32),
            pltpu.VMEM((heads, HD), F32),
            pltpu.VMEM((SPAN, SPAN), BF16),
            pltpu.VMEM((2 * nz, SPAN, HD), F32),
            pltpu.VMEM((2 * nz, SPAN, HD), F32),
            pltpu.VMEM((2, nz, HD, HD), BF16),
            pltpu.VMEM((2, nz, HD, HD), BF16),
            pltpu.VMEM((2, ns // 2, PIECE, HD), F32),
            pltpu.VMEM((ns, PIECE, HD), F32),
            pltpu.VMEM((ns, PIECE, HD), F32),
            pltpu.VMEM((2, HD, HD), F32),
            pltpu.VMEM((2, nz, HD, HD), BF16),
            pltpu.VMEM((2, nz, HD, HD), BF16),
            pltpu.VMEM((nz, SPAN, PAIR), BF16),
            pltpu.VMEM((2, PIECE, HD), F32),
            pltpu.VMEM((PIECE, HD), F32),
            pltpu.VMEM((2, HD), F32),
            pltpu.VMEM((nz, 8, HD), F32),
            pltpu.VMEM((nz, 8, HD), F32),
            pltpu.VMEM((2, PIECE, HD), F32),
            pltpu.VMEM((ns, PIECE, HD), F32),
            dma((3,)), dma((3, nz)), dma((3, nz)), dma((2,)),
            dma((2, 2, nz)), dma((2, 2, nz)), dma((2, ns // 2)), dma((ns,)), dma((ns,)), dma((2, ns // 2)),
            dma((2, 2, nz)), dma((2, 2, nz)), dma((nz,)), dma((nz,)), dma((nz,)), dma((2,)), dma((3,)),
            dma((nz,)), dma((nz,)), dma((ns,)), dma((ns,)),
        ],
        compiler_params=pltpu.CompilerParams(
            collective_id=0, has_side_effects=True, vmem_limit_bytes=60 * 1024 * 1024
        ),
        cost_estimate=pl.CostEstimate(flops=10**9, bytes_accessed=8 * 2**20, transcendentals=2 * 10**6),
    )(queries, keys, values, log_decay.T, cached_state, norm_gain)


def solution(mesh):
    rows = P(("seq", "head"), None)
    return jax.shard_map(
        functools.partial(local, mesh.shape["seq"], mesh.shape["head"] // 2),
        mesh=mesh,
        in_specs=(rows, rows, rows, rows, P("head", None, None), P("head", None)),
        out_specs=(rows, P("head", "seq", None)),
        check_vma=False,
    )
```

```python
import functools

import jax
import jax.numpy as jnp
from jax import lax
from jax.experimental import pallas as pl
from jax.experimental.pallas import tpu as pltpu
from jax.sharding import PartitionSpec as P

HD = 128
ROWS = 128
SPAN = 2 * ROWS
PAIR = 2 * HD
HALF = HD // 2
PIECE = 8
F32 = jnp.float32
BF16 = jnp.bfloat16
NEVER = -1e30
MESH = pl.DeviceIdType.MESH


def dot(a, b, dims=((1,), (0,))):
    return lax.dot_general(a, b, (dims, ((), ())), preferred_element_type=F32)


def kernel(
    ns, nz,
    q_ref, k_ref, v_ref, ld_ref, cached_ref, gain_ref,
    att_ref, fin_ref,
    tokens, ld_all, decay_rows, run_rows, fade_rows, end_rows, lower, run_all, within,
    l_send, l_recv, x_send, x_recv, e_send, e_recv, s_send, s_recv, out, fin_all, cached, gain, z_send, z_recv, d_send, d_recv,
    own_sem, in_send, in_recv, ld_sem, l_ss, l_rs, x_sem, e_sem, s_ss, s_rs, o_sem, f_sem, small_sem, z_sem, d_sem,
):
    seq = lax.axis_index("seq")
    head = lax.axis_index("head")
    z = lax.div(head, 2)
    core = lax.rem(head, 2)
    other = 1 - core
    partner = 2 * z + other
    group = lax.div(seq, 2)
    turn = lax.rem(seq, 2)
    sources = (k_ref, v_ref, q_ref)

    def columns(block, which):
        return pl.ds(pl.multiple_of((2 * block + which) * PAIR, PAIR), PAIR)

    def head_columns(block, u):
        return pl.ds(pl.multiple_of((2 * block + core) * PAIR + u * HD, HD), HD)

    def rows_of(a, block, u):
        at = head_columns(block, u)
        return jnp.concatenate([tokens[a, 0, :, at], tokens[a, 1, :, at]], axis=0)

    def near(t):
        step = lax.div(t + 1, 2)
        return lax.rem(z + jnp.where(lax.rem(t, 2) == 1, step, nz - step), nz)

    def order(t):
        return near(nz - 1 - t)

    def own_copy(a):
        return pltpu.make_async_copy(sources[a], tokens.at[a, core], own_sem.at[a])

    def to_partner(src, dst, ss, rs):
        return pltpu.make_async_remote_copy(
            src, dst, ss, rs, device_id=(seq, partner), device_id_type=MESH
        )

    def arrived(ref, sem):
        to_partner(ref, ref, sem, sem).wait_recv()

    def sent(ref, sem):
        to_partner(ref, ref, sem, sem).wait_send()

    def swap_copy(a, b):
        at = columns(b, other)
        landed = in_recv.at[nz] if a == 2 else in_recv.at[b]
        return to_partner(sources[a].at[:, at], tokens.at[a, core, :, at], in_send.at[0], landed)

    ld_copy = to_partner(ld_all.at[core], ld_all.at[core], ld_sem.at[0], ld_sem.at[1])
    ld_arrival = to_partner(ld_all.at[other], ld_all.at[other], ld_sem.at[0], ld_sem.at[1])

    part_rows = (pl.ds(0, HALF), pl.ds(HALF, HALF))
    near_ns = ns // 4

    def over_z(src, dst, ss, rs, u, part, to, slot, by_slot=False):
        return pltpu.make_async_remote_copy(
            src.at[u, to, part_rows[part]], dst.at[u, slot, part_rows[part]],
            ss.at[0], rs.at[3 + slot if by_slot and u == part == 1 else 2 * u + part],
            device_id=(seq, 2 * to + core), device_id_type=MESH,
        )

    def facts_copy(to, slot):
        return pltpu.make_async_remote_copy(
            z_send.at[to], z_recv.at[slot], z_sem.at[0], z_sem.at[1],
            device_id=(seq, 2 * to + core), device_id_type=MESH,
        )

    def decay_copy(to, slot):
        return pltpu.make_async_remote_copy(
            d_send.at[lax.rem(to, 2)], d_recv.at[slot], d_sem.at[0], d_sem.at[1],
            device_id=(to, head), device_id_type=MESH,
        )

    def piece_rows(g):
        return pl.ds(pl.multiple_of(g * PIECE, PIECE), PIECE)

    def sum_copy(u, g, slot):
        return pltpu.make_async_remote_copy(
            x_send.at[2 * g + u], x_recv.at[slot], x_sem.at[0], x_sem.at[1],
            device_id=(2 * g + u, head), device_id_type=MESH,
        )

    def entry_copy(u, g, to):
        return pltpu.make_async_remote_copy(
            e_send.at[to], e_recv.at[u, piece_rows(g)], e_sem.at[0], e_sem.at[1 + 2 * u + lax.div(g, near_ns)],
            device_id=(to, head), device_id_type=MESH,
        )

    barrier = pltpu.get_barrier_semaphore()
    pl.semaphore_signal(barrier, inc=1, device_id=(seq, partner), device_id_type=MESH)

    @pl.loop(1, nz)
    def _(t):
        pl.semaphore_signal(
            barrier, inc=1, device_id=(seq, 2 * lax.rem(z + t, nz) + core), device_id_type=MESH
        )

    @pl.loop(1, ns)
    def _(t):
        pl.semaphore_signal(barrier, inc=1, device_id=(lax.rem(seq + t, ns), head), device_id_type=MESH)

    ld_own = pltpu.make_async_copy(ld_ref, ld_all.at[core], small_sem.at[0])
    cached_own = pltpu.make_async_copy(cached_ref.at[turn, piece_rows(group)], cached, small_sem.at[1])
    gain_own = pltpu.make_async_copy(gain_ref, gain, small_sem.at[2])
    ld_own.start()
    for a in range(3):
        own_copy(a).start()
    cached_own.start()
    gain_own.start()
    causal = lax.broadcasted_iota(jnp.int32, (SPAN, SPAN), 0) >= lax.broadcasted_iota(jnp.int32, (SPAN, SPAN), 1)
    lower[...] = causal.astype(F32).astype(BF16)

    ld_own.wait()
    pl.semaphore_wait(barrier, 1 + (nz - 1) + (ns - 1))

    ld_copy.start()

    @pl.loop(0, nz)
    def _(t):
        for a in range(2):
            swap_copy(a, order(t)).start()

    halves = pl.ds(0, nz * PAIR)

    def swaps_done():
        ld_copy.wait_send()
        sent(tokens.at[:, 0, :, halves], in_send.at[0])

    ld_arrival.wait_recv()
    for half in range(2):
        decay_rows[:, half * ROWS : (half + 1) * ROWS] = ld_all[half].astype(F32)
    run = dot(decay_rows[...].astype(BF16), lower[...], ((1,), (1,)))
    run_rows[...] = run
    fade_rows[...] = jnp.exp(run[:, SPAN - 1 : SPAN] - run)
    end_rows[...] = jnp.broadcast_to(run[:, SPAN - 1 : SPAN], end_rows.shape)
    gain_own.wait()

    @pl.loop(0, nz)
    def _(t):
        b = order(t)
        first = 4 * b + 2 * core
        at = lax.broadcasted_iota(jnp.int32, (8, HD), 0)
        tile = jnp.where(at == 0, end_rows[pl.ds(first, 1), :], end_rows[pl.ds(first + 1, 1), :])
        z_send[b] = jnp.where(at < 2, tile, jnp.where(at == 2, gain[0:1, :], gain[1:2, :]))

        @pl.when(t < nz - 1)
        def _():
            facts_copy(b, z).start()

    z_recv[z] = z_send[z]
    for a in range(2):
        own_copy(a).wait()

    def send_part(u, part):
        @pl.loop(0, nz - 1)
        def _(t):
            over_z(l_send, l_recv, l_ss, l_rs, u, part, order(t), z).start()

    for u in range(2):
        @pl.loop(0, nz)
        def _(t):
            b = order(t)
            if u == 0:
                arrived(tokens.at[pl.ds(0, 2), other, :, columns(b, core)], in_recv.at[b])
            which = pl.ds(4 * b + 2 * core + u, 1)
            scaled = rows_of(0, b, u).T.astype(F32) * fade_rows[which, :]
            high = scaled.astype(BF16)
            low = (scaled - high.astype(F32)).astype(BF16)
            both = dot(jnp.concatenate([high, low], axis=0), rows_of(1, b, u))
            state = (both[:HD] + both[HD:]).astype(BF16)
            l_send[u, b] = state

            @pl.when(t < nz - 1)
            def _():
                over_z(l_send, l_recv, l_ss, l_rs, u, 0, b, z).start()

        send_part(u, 1)
        l_recv[u, z] = l_send[u, z]
        if u == 0:
            @pl.loop(0, nz)
            def _(t):
                swap_copy(2, t).start()

            arrived(z_recv.at[pl.ds(0, nz - 1)], z_sem.at[1])
            total = lax.fori_loop(0, nz, lambda b, sums: sums + z_recv[b], jnp.zeros((8, HD), F32))
            for v in range(2):
                d_send[v] = jnp.broadcast_to(total[v : v + 1], (PIECE, HD))

            @pl.loop(1, ns)
            def _(t):
                decay_copy(lax.rem(seq + t, ns), seq).start()

            d_recv[seq] = d_send[turn]

    def l_done():
        sent(l_send.at[:, pl.ds(0, nz - 1)], l_ss.at[0])

    own_copy(2).wait()
    arrived(tokens.at[2, other, :, halves], in_recv.at[nz])

    def inside(b):
        for u in range(2):
            which = pl.ds(4 * b + 2 * core + u, 1)
            token = jnp.broadcast_to(decay_rows[which, :], (HD, SPAN)).astype(BF16)
            run = dot(lower[...], token, ((1,), (1,)))
            run_all[2 * b + u] = run
            scores = dot(rows_of(2, b, u), rows_of(0, b, u), ((1,), (1,)))
            gap = jnp.concatenate([run, run], axis=1) - run_rows[which, :]
            here = (
                lax.broadcasted_iota(jnp.int32, (SPAN, SPAN), 0)
                >= lax.broadcasted_iota(jnp.int32, (SPAN, SPAN), 1)
            )
            weights = (scores * jnp.exp(jnp.where(here, gap, NEVER))).astype(BF16)
            within[2 * b + u] = dot(weights, rows_of(1, b, u))

    pl.loop(0, nz // 2)(inside)

    def column_sum(u, part):
        arrived(l_recv.at[u, pl.ds(0, nz - 1), part_rows[part]], l_rs.at[2 * u + part])

        def add(b, sums):
            return jnp.exp(z_recv[b, u : u + 1, :]) * sums + l_recv[u, b, part_rows[part], :].astype(F32)

        state = lax.fori_loop(0, nz, add, jnp.zeros((HALF, HD), F32))
        for g in range(near_ns):
            x_send[2 * (near_ns * part + g) + u] = state[PIECE * g : PIECE * (g + 1)]

        @pl.loop(0, near_ns)
        def _(t):
            g = near_ns * part + lax.rem(group + 1 + t, near_ns)

            @pl.when(2 * g + u != seq)
            def _():
                sum_copy(u, g, seq).start()

        @pl.when((turn == u) & (lax.div(group, near_ns) == part))
        def _():
            x_recv[seq] = x_send[seq]

    def columns_scan(u, part):
        @pl.when((turn == u) & (lax.div(group, near_ns) == part))
        def _():
            arrived(x_recv.at[pl.ds(0, ns - 1)], x_sem.at[1])
            piece = cached[...]
            for i in range(ns):
                e_send[i] = piece
                piece = jnp.exp(d_recv[i]) * piece + x_recv[i]
            fin_all[u] = piece

            @pl.loop(0, ns)
            def _(t):
                i = lax.rem(seq + t + 3 * ns // 8, ns)

                @pl.when(i != seq)
                def _():
                    entry_copy(u, group, i).start()

            e_recv[u, piece_rows(group), :] = e_send[seq]

    def give(u, part):
        landed = e_sem.at[1 + 2 * u + part]
        owner = (turn == u) & (lax.div(group, near_ns) == part)

        @pl.when(owner)
        def _():
            arrived(e_recv.at[u, pl.ds(0, HALF - PIECE)], landed)

        @pl.when(jnp.logical_not(owner))
        def _():
            arrived(e_recv.at[u, pl.ds(0, HALF)], landed)

        def step(b, state):
            s_send[u, b, part_rows[part], :] = state.astype(BF16)
            return jnp.exp(z_recv[b, u : u + 1, :]) * state + l_recv[u, b, part_rows[part], :].astype(F32)

        lax.fori_loop(0, nz, step, e_recv[u, HALF * part : HALF * (part + 1), :])

        @pl.loop(0, nz - 1)
        def _(t):
            over_z(s_send, s_recv, s_ss, s_rs, u, part, order(t), z, True).start()

        if part == 1:
            s_recv[u, z] = s_send[u, z]

    column_sum(0, 0)
    column_sum(0, 1)
    pl.loop(nz // 2, nz)(inside)
    cached_own.wait()

    arrived(d_recv.at[pl.ds(0, ns - 1)], d_sem.at[1])

    columns_scan(0, 0)
    column_sum(1, 0)
    columns_scan(0, 1)
    column_sum(1, 1)
    give(0, 0)
    columns_scan(1, 0)
    give(0, 1)
    columns_scan(1, 1)
    give(1, 0)
    swaps_done()
    l_done()
    give(1, 1)

    def scan_done():
        sent(x_send.at[pl.ds(0, ns - 1)], x_sem.at[0])
        sent(e_send.at[pl.ds(0, ns - 1)], e_sem.at[0])
        sent(d_recv.at[pl.ds(0, ns - 1)], d_sem.at[0])
        sent(z_send.at[pl.ds(0, nz - 1)], z_sem.at[0])

    def s_done():
        sent(s_send.at[:, pl.ds(0, nz - 1)], s_ss.at[0])

    def fin_copy(slot):
        return pltpu.make_async_remote_copy(
            fin_all.at[slot], fin_all.at[slot], f_sem.at[0], f_sem.at[1],
            device_id=(2 * group + 1 - turn, head), device_id_type=MESH,
        )

    fin_copy(turn).start()

    mine_rows = pl.ds(pl.multiple_of(core * ROWS, ROWS), ROWS)
    other_rows = pl.ds(pl.multiple_of(other * ROWS, ROWS), ROWS)

    def out_own(b):
        return pltpu.make_async_copy(out.at[b, mine_rows], att_ref.at[:, columns(b, core)], o_sem.at[0])

    def out_swap(b):
        return to_partner(out.at[b, other_rows], att_ref.at[:, columns(b, core)], o_sem.at[1], o_sem.at[2])

    def output(u):
        for part in range(2 - u):
            arrived(s_recv.at[u, pl.ds(0, nz - 1), part_rows[part]], s_rs.at[2 * u + part])

        @pl.loop(0, nz)
        def _(t):
            b = near(t)

            if u == 1:
                @pl.when(t > 0)
                def _():
                    arrived(s_recv.at[u, b, part_rows[1]], s_rs.at[3 + b])

            carried = dot(rows_of(2, b, u), s_recv[u, b])
            mixed = within[2 * b + u] + carried * jnp.exp(run_all[2 * b + u])
            mean = jnp.mean(mixed * mixed, axis=1, keepdims=True)
            normed = mixed * lax.rsqrt(mean + 1e-6) * z_recv[b, 2 + u : 3 + u, :]
            out[b, :, u * HD : (u + 1) * HD] = normed.astype(BF16)
            if u == 1:
                out_own(b).start()
                out_swap(b).start()

    output(0)
    scan_done()
    output(1)
    fin_copy(1 - turn).wait_recv()
    for u in range(2):
        fin_ref[u] = jnp.where(turn == 0, fin_all[u, 0:4, :], fin_all[u, 4:8, :])

    fin_copy(turn).wait_send()
    s_done()

    some = out.at[:, pl.ds(0, ROWS)]
    pltpu.make_async_copy(some, some, o_sem.at[0]).wait()
    sent(some, o_sem.at[1])
    arrived(some, o_sem.at[2])


def local(ns, nz, queries, keys, values, log_decay, cached_state, norm_gain):
    anywhere = pl.BlockSpec(memory_space=pl.ANY)
    vmem = pl.BlockSpec(memory_space=pltpu.VMEM)
    dma = pltpu.SemaphoreType.DMA
    heads = log_decay.shape[1]
    return pl.pallas_call(
        functools.partial(kernel, ns, nz),
        out_shape=(
            jax.ShapeDtypeStruct(queries.shape, BF16),
            jax.ShapeDtypeStruct((2, HD // ns, HD), F32),
        ),
        in_specs=[anywhere] * 6,
        out_specs=(anywhere, vmem),
        scratch_shapes=[
            pltpu.VMEM((3, 2) + queries.shape, BF16),
            pltpu.VMEM((2, heads, ROWS), BF16),
            pltpu.VMEM((heads, SPAN), F32),
            pltpu.VMEM((heads, SPAN), F32),
            pltpu.VMEM((heads, SPAN), F32),
            pltpu.VMEM((heads, HD), F32),
            pltpu.VMEM((SPAN, SPAN), BF16),
            pltpu.VMEM((2 * nz, SPAN, HD), F32),
            pltpu.VMEM((2 * nz, SPAN, HD), F32),
            pltpu.VMEM((2, nz, HD, HD), BF16),
            pltpu.VMEM((2, nz, HD, HD), BF16),
            pltpu.VMEM((ns, PIECE, HD), F32),
            pltpu.VMEM((ns, PIECE, HD), F32),
            pltpu.VMEM((ns, PIECE, HD), F32),
            pltpu.VMEM((2, HD, HD), F32),
            pltpu.VMEM((2, nz, HD, HD), BF16),
            pltpu.VMEM((2, nz, HD, HD), BF16),
            pltpu.VMEM((nz, SPAN, PAIR), BF16),
            pltpu.VMEM((2, PIECE, HD), F32),
            pltpu.VMEM((PIECE, HD), F32),
            pltpu.VMEM((2, HD), F32),
            pltpu.VMEM((nz, 8, HD), F32),
            pltpu.VMEM((nz, 8, HD), F32),
            pltpu.VMEM((2, PIECE, HD), F32),
            pltpu.VMEM((ns, PIECE, HD), F32),
            dma((3,)), dma((1,)), dma((nz + 1,)), dma((2,)),
            dma((1,)), dma((4,)), dma((2,)), dma((5,)), dma((1,)), dma((3 + nz,)),
            dma((3,)), dma((2,)), dma((3,)), dma((2,)), dma((2,)),
        ],
        compiler_params=pltpu.CompilerParams(
            collective_id=0, has_side_effects=True, vmem_limit_bytes=60 * 1024 * 1024
        ),
        cost_estimate=pl.CostEstimate(flops=10**9, bytes_accessed=8 * 2**20, transcendentals=2 * 10**6),
    )(queries, keys, values, log_decay.T, cached_state, norm_gain)


def solution(mesh):
    rows = P(("seq", "head"), None)
    return jax.shard_map(
        functools.partial(local, mesh.shape["seq"], mesh.shape["head"] // 2),
        mesh=mesh,
        in_specs=(rows, rows, rows, rows, P("head", None, None), P("head", None)),
        out_specs=(rows, P("head", "seq", None)),
        check_vma=False,
    )
```

```python
import functools

import jax
import jax.numpy as jnp
from jax import lax
from jax.experimental import pallas as pl
from jax.experimental.pallas import tpu as pltpu
from jax.sharding import PartitionSpec as P

HD = 128
ROWS = 128
SPAN = 2 * ROWS
PAIR = 2 * HD
HALF = HD // 2
PIECE = 8
F32 = jnp.float32
BF16 = jnp.bfloat16
NEVER = -1e30
MESH = pl.DeviceIdType.MESH


def dot(a, b, dims=((1,), (0,))):
    return lax.dot_general(a, b, (dims, ((), ())), preferred_element_type=F32)


def kernel(
    ns, nz,
    q_ref, k_ref, v_ref, ld_ref, cached_ref, gain_ref,
    att_ref, fin_ref,
    tokens, ld_all, decay_rows, run_rows, fade_rows, end_rows, lower, run_all, within,
    l_send, l_recv, x_send, x_recv, e_send, e_recv, s_send, s_recv, out, fin_all, cached, gain, z_send, z_recv, d_send, d_recv,
    own_sem, in_send, in_recv, ld_sem, l_ss, l_rs, x_sem, e_sem, s_ss, s_rs, o_sem, f_sem, small_sem, z_sem, d_sem,
):
    seq = lax.axis_index("seq")
    head = lax.axis_index("head")
    z = lax.div(head, 2)
    core = lax.rem(head, 2)
    other = 1 - core
    partner = 2 * z + other
    group = lax.div(seq, 2)
    turn = lax.rem(seq, 2)
    sources = (k_ref, v_ref, q_ref)

    def columns(block, which):
        return pl.ds(pl.multiple_of((2 * block + which) * PAIR, PAIR), PAIR)

    def head_columns(block, u):
        return pl.ds(pl.multiple_of((2 * block + core) * PAIR + u * HD, HD), HD)

    def rows_of(a, block, u):
        at = head_columns(block, u)
        return jnp.concatenate([tokens[a, 0, :, at], tokens[a, 1, :, at]], axis=0)

    def near(t):
        step = lax.div(t + 1, 2)
        return lax.rem(z + jnp.where(lax.rem(t, 2) == 1, step, nz - step), nz)

    def order(t):
        return near(nz - 1 - t)

    def own_copy(a):
        return pltpu.make_async_copy(sources[a], tokens.at[a, core], own_sem.at[a])

    def to_partner(src, dst, ss, rs):
        return pltpu.make_async_remote_copy(
            src, dst, ss, rs, device_id=(seq, partner), device_id_type=MESH
        )

    def arrived(ref, sem):
        to_partner(ref, ref, sem, sem).wait_recv()

    def sent(ref, sem):
        to_partner(ref, ref, sem, sem).wait_send()

    def swap_copy(a, b):
        at = columns(b, other)
        landed = in_recv.at[nz] if a == 2 else in_recv.at[b]
        return to_partner(sources[a].at[:, at], tokens.at[a, core, :, at], in_send.at[0], landed)

    ld_copy = to_partner(ld_all.at[core], ld_all.at[core], ld_sem.at[0], ld_sem.at[1])
    ld_arrival = to_partner(ld_all.at[other], ld_all.at[other], ld_sem.at[0], ld_sem.at[1])

    part_rows = (pl.ds(0, HALF), pl.ds(HALF, HALF))
    near_ns = ns // 4

    def over_z(src, dst, ss, rs, u, part, to, slot, by_slot=False):
        return pltpu.make_async_remote_copy(
            src.at[u, to, part_rows[part]], dst.at[u, slot, part_rows[part]],
            ss.at[0], rs.at[3 + slot if by_slot and u == part == 1 else 2 * u + part],
            device_id=(seq, 2 * to + core), device_id_type=MESH,
        )

    def facts_copy(to, slot):
        return pltpu.make_async_remote_copy(
            z_send.at[to], z_recv.at[slot], z_sem.at[0], z_sem.at[1],
            device_id=(seq, 2 * to + core), device_id_type=MESH,
        )

    def decay_copy(to, slot):
        return pltpu.make_async_remote_copy(
            d_send.at[lax.rem(to, 2)], d_recv.at[slot], d_sem.at[0], d_sem.at[1],
            device_id=(to, head), device_id_type=MESH,
        )

    def piece_rows(g):
        return pl.ds(pl.multiple_of(g * PIECE, PIECE), PIECE)

    def sum_copy(u, g, slot):
        return pltpu.make_async_remote_copy(
            x_send.at[2 * g + u], x_recv.at[slot], x_sem.at[0], x_sem.at[1],
            device_id=(2 * g + u, head), device_id_type=MESH,
        )

    def entry_copy(u, g, to):
        return pltpu.make_async_remote_copy(
            e_send.at[to], e_recv.at[u, piece_rows(g)], e_sem.at[0], e_sem.at[1 + 2 * u + lax.div(g, near_ns)],
            device_id=(to, head), device_id_type=MESH,
        )

    barrier = pltpu.get_barrier_semaphore()
    pl.semaphore_signal(barrier, inc=1, device_id=(seq, partner), device_id_type=MESH)

    @pl.loop(1, nz)
    def _(t):
        pl.semaphore_signal(
            barrier, inc=1, device_id=(seq, 2 * lax.rem(z + t, nz) + core), device_id_type=MESH
        )

    @pl.loop(1, ns)
    def _(t):
        pl.semaphore_signal(barrier, inc=1, device_id=(lax.rem(seq + t, ns), head), device_id_type=MESH)

    ld_own = pltpu.make_async_copy(ld_ref, ld_all.at[core], small_sem.at[0])
    cached_own = pltpu.make_async_copy(cached_ref.at[turn, piece_rows(group)], cached, small_sem.at[1])
    gain_own = pltpu.make_async_copy(gain_ref, gain, small_sem.at[2])
    ld_own.start()
    for a in range(3):
        own_copy(a).start()
    cached_own.start()
    gain_own.start()
    causal = lax.broadcasted_iota(jnp.int32, (SPAN, SPAN), 0) >= lax.broadcasted_iota(jnp.int32, (SPAN, SPAN), 1)
    lower[...] = causal.astype(F32).astype(BF16)

    ld_own.wait()
    pl.semaphore_wait(barrier, 1 + (nz - 1) + (ns - 1))

    ld_copy.start()

    @pl.loop(0, nz)
    def _(t):
        for a in range(2):
            swap_copy(a, order(t)).start()

    halves = pl.ds(0, nz * PAIR)

    def swaps_done():
        ld_copy.wait_send()
        sent(tokens.at[:, 0, :, halves], in_send.at[0])

    ld_arrival.wait_recv()
    for half in range(2):
        decay_rows[:, half * ROWS : (half + 1) * ROWS] = ld_all[half].astype(F32)
    run = dot(decay_rows[...].astype(BF16), lower[...], ((1,), (1,)))
    run_rows[...] = run
    fade_rows[...] = jnp.exp(run[:, SPAN - 1 : SPAN] - run)
    end_rows[...] = jnp.broadcast_to(run[:, SPAN - 1 : SPAN], end_rows.shape)
    gain_own.wait()

    @pl.loop(0, nz)
    def _(t):
        b = order(t)
        first = 4 * b + 2 * core
        at = lax.broadcasted_iota(jnp.int32, (8, HD), 0)
        tile = jnp.where(at == 0, end_rows[pl.ds(first, 1), :], end_rows[pl.ds(first + 1, 1), :])
        z_send[b] = jnp.where(at < 2, tile, jnp.where(at == 2, gain[0:1, :], gain[1:2, :]))

        @pl.when(t < nz - 1)
        def _():
            facts_copy(b, z).start()

    z_recv[z] = z_send[z]
    for a in range(2):
        own_copy(a).wait()

    def send_part(u, part):
        @pl.loop(0, nz - 1)
        def _(t):
            over_z(l_send, l_recv, l_ss, l_rs, u, part, order(t), z).start()

    for u in range(2):
        @pl.loop(0, nz)
        def _(t):
            b = order(t)
            if u == 0:
                arrived(tokens.at[pl.ds(0, 2), other, :, columns(b, core)], in_recv.at[b])
            which = pl.ds(4 * b + 2 * core + u, 1)
            scaled = rows_of(0, b, u).T.astype(F32) * fade_rows[which, :]
            high = scaled.astype(BF16)
            low = (scaled - high.astype(F32)).astype(BF16)
            both = dot(jnp.concatenate([high, low], axis=0), rows_of(1, b, u))
            state = (both[:HD] + both[HD:]).astype(BF16)
            l_send[u, b] = state

            @pl.when(t < nz - 1)
            def _():
                over_z(l_send, l_recv, l_ss, l_rs, u, 0, b, z).start()

        send_part(u, 1)
        l_recv[u, z] = l_send[u, z]

        if u == 1:
            @pl.loop(0, nz)
            def _(t):
                swap_copy(2, t).start()

            arrived(z_recv.at[pl.ds(0, nz - 1)], z_sem.at[1])
            total = lax.fori_loop(0, nz, lambda b, sums: sums + z_recv[b], jnp.zeros((8, HD), F32))
            for v in range(2):
                d_send[v] = jnp.broadcast_to(total[v : v + 1], (PIECE, HD))

            @pl.loop(1, ns)
            def _(t):
                decay_copy(lax.rem(seq + t, ns), seq).start()

            d_recv[seq] = d_send[turn]

    def l_done():
        sent(l_send.at[:, pl.ds(0, nz - 1)], l_ss.at[0])

    own_copy(2).wait()
    arrived(tokens.at[2, other, :, halves], in_recv.at[nz])

    def inside(b):
        for u in range(2):
            which = pl.ds(4 * b + 2 * core + u, 1)
            token = jnp.broadcast_to(decay_rows[which, :], (HD, SPAN)).astype(BF16)
            run = dot(lower[...], token, ((1,), (1,)))
            run_all[2 * b + u] = run
            scores = dot(rows_of(2, b, u), rows_of(0, b, u), ((1,), (1,)))
            gap = jnp.concatenate([run, run], axis=1) - run_rows[which, :]
            here = (
                lax.broadcasted_iota(jnp.int32, (SPAN, SPAN), 0)
                >= lax.broadcasted_iota(jnp.int32, (SPAN, SPAN), 1)
            )
            weights = (scores * jnp.exp(jnp.where(here, gap, NEVER))).astype(BF16)
            within[2 * b + u] = dot(weights, rows_of(1, b, u))


    def column_sum(u, part):
        arrived(l_recv.at[u, pl.ds(0, nz - 1), part_rows[part]], l_rs.at[2 * u + part])

        def add(b, sums):
            return jnp.exp(z_recv[b, u : u + 1, :]) * sums + l_recv[u, b, part_rows[part], :].astype(F32)

        state = lax.fori_loop(0, nz, add, jnp.zeros((HALF, HD), F32))
        for g in range(near_ns):
            x_send[2 * (near_ns * part + g) + u] = state[PIECE * g : PIECE * (g + 1)]

        @pl.loop(0, near_ns)
        def _(t):
            g = near_ns * part + lax.rem(group + 1 + t, near_ns)

            @pl.when(2 * g + u != seq)
            def _():
                sum_copy(u, g, seq).start()

        @pl.when((turn == u) & (lax.div(group, near_ns) == part))
        def _():
            x_recv[seq] = x_send[seq]

    def columns_scan(u, part):
        @pl.when((turn == u) & (lax.div(group, near_ns) == part))
        def _():
            arrived(x_recv.at[pl.ds(0, ns - 1)], x_sem.at[1])
            piece = cached[...]
            for i in range(ns):
                e_send[i] = piece
                piece = jnp.exp(d_recv[i]) * piece + x_recv[i]
            fin_all[u] = piece

            @pl.loop(0, ns)
            def _(t):
                i = lax.rem(seq + t + 3 * ns // 8, ns)

                @pl.when(i != seq)
                def _():
                    entry_copy(u, group, i).start()

            e_recv[u, piece_rows(group), :] = e_send[seq]

    def give(u, part):
        landed = e_sem.at[1 + 2 * u + part]
        owner = (turn == u) & (lax.div(group, near_ns) == part)

        @pl.when(owner)
        def _():
            arrived(e_recv.at[u, pl.ds(0, HALF - PIECE)], landed)

        @pl.when(jnp.logical_not(owner))
        def _():
            arrived(e_recv.at[u, pl.ds(0, HALF)], landed)

        def step(b, state):
            s_send[u, b, part_rows[part], :] = state.astype(BF16)

            @pl.when(b != z)
            def _():
                over_z(s_send, s_recv, s_ss, s_rs, u, part, b, z, True).start()

            return jnp.exp(z_recv[b, u : u + 1, :]) * state + l_recv[u, b, part_rows[part], :].astype(F32)

        lax.fori_loop(0, nz, step, e_recv[u, HALF * part : HALF * (part + 1), :])

        if part == 1:
            s_recv[u, z] = s_send[u, z]

    column_sum(0, 0)
    pl.loop(0 * nz // 8, 2 * nz // 8)(inside)
    column_sum(0, 1)
    pl.loop(2 * nz // 8, 4 * nz // 8)(inside)
    column_sum(1, 0)
    cached_own.wait()
    arrived(d_recv.at[pl.ds(0, ns - 1)], d_sem.at[1])
    columns_scan(0, 0)
    column_sum(1, 1)
    columns_scan(0, 1)
    pl.loop(4 * nz // 8, 8 * nz // 8)(inside)
    give(0, 0)
    columns_scan(1, 0)
    give(0, 1)
    columns_scan(1, 1)
    give(1, 0)
    swaps_done()
    l_done()
    give(1, 1)

    def scan_done():
        sent(x_send.at[pl.ds(0, ns - 1)], x_sem.at[0])
        sent(e_send.at[pl.ds(0, ns - 1)], e_sem.at[0])
        sent(d_recv.at[pl.ds(0, ns - 1)], d_sem.at[0])
        sent(z_send.at[pl.ds(0, nz - 1)], z_sem.at[0])

    def s_done():
        sent(s_send.at[:, pl.ds(0, nz - 1)], s_ss.at[0])

    def fin_copy(slot):
        return pltpu.make_async_remote_copy(
            fin_all.at[slot], fin_all.at[slot], f_sem.at[0], f_sem.at[1],
            device_id=(2 * group + 1 - turn, head), device_id_type=MESH,
        )

    fin_copy(turn).start()

    mine_rows = pl.ds(pl.multiple_of(core * ROWS, ROWS), ROWS)
    other_rows = pl.ds(pl.multiple_of(other * ROWS, ROWS), ROWS)

    def out_own(b):
        return pltpu.make_async_copy(out.at[b, mine_rows], att_ref.at[:, columns(b, core)], o_sem.at[0])

    def out_swap(b):
        return to_partner(out.at[b, other_rows], att_ref.at[:, columns(b, core)], o_sem.at[1], o_sem.at[2])

    def output(u):
        for part in range(2 - u):
            arrived(s_recv.at[u, pl.ds(0, nz - 1), part_rows[part]], s_rs.at[2 * u + part])

        @pl.loop(0, nz)
        def _(t):
            b = near(t)

            if u == 1:
                @pl.when(t > 0)
                def _():
                    arrived(s_recv.at[u, b, part_rows[1]], s_rs.at[3 + b])

            carried = dot(rows_of(2, b, u), s_recv[u, b])
            mixed = within[2 * b + u] + carried * jnp.exp(run_all[2 * b + u])
            mean = jnp.mean(mixed * mixed, axis=1, keepdims=True)
            normed = mixed * lax.rsqrt(mean + 1e-6) * z_recv[b, 2 + u : 3 + u, :]
            out[b, :, u * HD : (u + 1) * HD] = normed.astype(BF16)
            if u == 1:
                out_own(b).start()
                out_swap(b).start()

    output(0)
    scan_done()
    output(1)
    fin_copy(1 - turn).wait_recv()
    for u in range(2):
        fin_ref[u] = jnp.where(turn == 0, fin_all[u, 0:4, :], fin_all[u, 4:8, :])

    fin_copy(turn).wait_send()
    s_done()

    some = out.at[:, pl.ds(0, ROWS)]
    pltpu.make_async_copy(some, some, o_sem.at[0]).wait()
    sent(some, o_sem.at[1])
    arrived(some, o_sem.at[2])


def local(ns, nz, queries, keys, values, log_decay, cached_state, norm_gain):
    anywhere = pl.BlockSpec(memory_space=pl.ANY)
    vmem = pl.BlockSpec(memory_space=pltpu.VMEM)
    dma = pltpu.SemaphoreType.DMA
    heads = log_decay.shape[1]
    return pl.pallas_call(
        functools.partial(kernel, ns, nz),
        out_shape=(
            pltpu.VMEM(queries.shape, BF16),
            pltpu.VMEM((2, HD // ns, HD), F32),
        ),
        in_specs=[anywhere] * 6,
        out_specs=(anywhere, vmem),
        scratch_shapes=[
            pltpu.VMEM((3, 2) + queries.shape, BF16),
            pltpu.VMEM((2, heads, ROWS), BF16),
            pltpu.VMEM((heads, SPAN), F32),
            pltpu.VMEM((heads, SPAN), F32),
            pltpu.VMEM((heads, SPAN), F32),
            pltpu.VMEM((heads, HD), F32),
            pltpu.VMEM((SPAN, SPAN), BF16),
            pltpu.VMEM((2 * nz, SPAN, HD), F32),
            pltpu.VMEM((2 * nz, SPAN, HD), F32),
            pltpu.VMEM((2, nz, HD, HD), BF16),
            pltpu.VMEM((2, nz, HD, HD), BF16),
            pltpu.VMEM((ns, PIECE, HD), F32),
            pltpu.VMEM((ns, PIECE, HD), F32),
            pltpu.VMEM((ns, PIECE, HD), F32),
            pltpu.VMEM((2, HD, HD), F32),
            pltpu.VMEM((2, nz, HD, HD), BF16),
            pltpu.VMEM((2, nz, HD, HD), BF16),
            pltpu.VMEM((nz, SPAN, PAIR), BF16),
            pltpu.VMEM((2, PIECE, HD), F32),
            pltpu.VMEM((PIECE, HD), F32),
            pltpu.VMEM((2, HD), F32),
            pltpu.VMEM((nz, 8, HD), F32),
            pltpu.VMEM((nz, 8, HD), F32),
            pltpu.VMEM((2, PIECE, HD), F32),
            pltpu.VMEM((ns, PIECE, HD), F32),
            dma((3,)), dma((1,)), dma((nz + 1,)), dma((2,)),
            dma((1,)), dma((4,)), dma((2,)), dma((5,)), dma((1,)), dma((3 + nz,)),
            dma((3,)), dma((2,)), dma((3,)), dma((2,)), dma((2,)),
        ],
        compiler_params=pltpu.CompilerParams(
            collective_id=0, has_side_effects=True, vmem_limit_bytes=58 * 1024 * 1024
        ),
        cost_estimate=pl.CostEstimate(flops=10**9, bytes_accessed=8 * 2**20, transcendentals=2 * 10**6),
    )(queries, keys, values, log_decay.T, cached_state, norm_gain)


def solution(mesh):
    rows = P(("seq", "head"), None)
    return jax.shard_map(
        functools.partial(local, mesh.shape["seq"], mesh.shape["head"] // 2),
        mesh=mesh,
        in_specs=(rows, rows, rows, rows, P("head", None, None), P("head", None)),
        out_specs=(rows, P("head", "seq", None)),
        check_vma=False,
    )
```

```python
import functools

import jax
import jax.numpy as jnp
from jax import lax
from jax.experimental import pallas as pl
from jax.experimental.pallas import tpu as pltpu
from jax.sharding import PartitionSpec as P

HD = 128
ROWS = 128
SPAN = 2 * ROWS
PAIR = 2 * HD
HALF = HD // 2
PIECE = 8
F32 = jnp.float32
BF16 = jnp.bfloat16
NEVER = -1e30
MESH = pl.DeviceIdType.MESH


def dot(a, b, dims=((1,), (0,))):
    return lax.dot_general(a, b, (dims, ((), ())), preferred_element_type=F32)


def kernel(
    ns, nz,
    q_ref, k_ref, v_ref, ld_ref, cached_ref, gain_ref,
    att_ref, fin_ref,
    tokens, ld_all, decay_rows, run_rows, fade_rows, end_rows, lower, run_all, within,
    l_send, l_recv, x_send, x_recv, e_send, e_recv, s_send, s_recv, out, fin_all, cached, gain, z_send, z_recv, d_send, d_recv,
    own_sem, in_send, in_recv, ld_sem, l_ss, l_rs, x_sem, e_sem, s_ss, s_rs, o_sem, f_sem, small_sem, z_sem, d_sem,
):
    seq = lax.axis_index("seq")
    head = lax.axis_index("head")
    z = lax.div(head, 2)
    core = lax.rem(head, 2)
    other = 1 - core
    partner = 2 * z + other
    group = lax.div(seq, 2)
    turn = lax.rem(seq, 2)
    sources = (k_ref, v_ref, q_ref)

    def columns(block, which):
        return pl.ds(pl.multiple_of((2 * block + which) * PAIR, PAIR), PAIR)

    def head_columns(block, u):
        return pl.ds(pl.multiple_of((2 * block + core) * PAIR + u * HD, HD), HD)

    def rows_of(a, block, u):
        at = head_columns(block, u)
        return jnp.concatenate([tokens[a, 0, :, at], tokens[a, 1, :, at]], axis=0)

    def near(t):
        step = lax.div(t + 1, 2)
        return lax.rem(z + jnp.where(lax.rem(t, 2) == 1, step, nz - step), nz)

    def order(t):
        return near(nz - 1 - t)

    def own_copy(a):
        return pltpu.make_async_copy(sources[a], tokens.at[a, core], own_sem.at[a])

    def to_partner(src, dst, ss, rs):
        return pltpu.make_async_remote_copy(
            src, dst, ss, rs, device_id=(seq, partner), device_id_type=MESH
        )

    def arrived(ref, sem):
        to_partner(ref, ref, sem, sem).wait_recv()

    def sent(ref, sem):
        to_partner(ref, ref, sem, sem).wait_send()

    def swap_copy(a, b):
        at = columns(b, other)
        landed = in_recv.at[nz] if a == 2 else in_recv.at[b]
        return to_partner(sources[a].at[:, at], tokens.at[a, core, :, at], in_send.at[0], landed)

    ld_copy = to_partner(ld_all.at[core], ld_all.at[core], ld_sem.at[0], ld_sem.at[1])
    ld_arrival = to_partner(ld_all.at[other], ld_all.at[other], ld_sem.at[0], ld_sem.at[1])

    part_rows = (pl.ds(0, HALF), pl.ds(HALF, HALF))
    near_ns = ns // 4

    def over_z(src, dst, ss, rs, u, part, to, slot, by_slot=False):
        return pltpu.make_async_remote_copy(
            src.at[u, to, part_rows[part]], dst.at[u, slot, part_rows[part]],
            ss.at[0], rs.at[3 + slot if by_slot and u == part == 1 else 2 * u + part],
            device_id=(seq, 2 * to + core), device_id_type=MESH,
        )

    def facts_copy(to, slot):
        return pltpu.make_async_remote_copy(
            z_send.at[to], z_recv.at[slot], z_sem.at[0], z_sem.at[1],
            device_id=(seq, 2 * to + core), device_id_type=MESH,
        )

    def decay_copy(to, slot):
        return pltpu.make_async_remote_copy(
            d_send.at[lax.rem(to, 2)], d_recv.at[slot], d_sem.at[0], d_sem.at[1],
            device_id=(to, head), device_id_type=MESH,
        )

    def piece_rows(g):
        return pl.ds(pl.multiple_of(g * PIECE, PIECE), PIECE)

    def sum_copy(u, g, slot):
        return pltpu.make_async_remote_copy(
            x_send.at[2 * g + u], x_recv.at[slot], x_sem.at[0], x_sem.at[1],
            device_id=(2 * g + u, head), device_id_type=MESH,
        )

    def entry_copy(u, g, to):
        return pltpu.make_async_remote_copy(
            e_send.at[to], e_recv.at[u, piece_rows(g)], e_sem.at[0], e_sem.at[1 + 2 * u + lax.div(g, near_ns)],
            device_id=(to, head), device_id_type=MESH,
        )

    barrier = pltpu.get_barrier_semaphore()
    pl.semaphore_signal(barrier, inc=1, device_id=(seq, partner), device_id_type=MESH)

    @pl.loop(1, nz)
    def _(t):
        pl.semaphore_signal(
            barrier, inc=1, device_id=(seq, 2 * lax.rem(z + t, nz) + core), device_id_type=MESH
        )

    @pl.loop(1, ns)
    def _(t):
        pl.semaphore_signal(barrier, inc=1, device_id=(lax.rem(seq + t, ns), head), device_id_type=MESH)

    ld_own = pltpu.make_async_copy(ld_ref, ld_all.at[core], small_sem.at[0])
    cached_own = pltpu.make_async_copy(cached_ref.at[turn, piece_rows(group)], cached, small_sem.at[1])
    gain_own = pltpu.make_async_copy(gain_ref, gain, small_sem.at[2])
    ld_own.start()
    for a in range(3):
        own_copy(a).start()
    cached_own.start()
    gain_own.start()
    causal = lax.broadcasted_iota(jnp.int32, (SPAN, SPAN), 0) >= lax.broadcasted_iota(jnp.int32, (SPAN, SPAN), 1)
    lower[...] = causal.astype(F32).astype(BF16)

    ld_own.wait()
    pl.semaphore_wait(barrier, 1 + (nz - 1) + (ns - 1))

    ld_copy.start()

    @pl.loop(0, nz)
    def _(t):
        for a in range(2):
            swap_copy(a, order(t)).start()

    halves = pl.ds(0, nz * PAIR)

    def swaps_done():
        ld_copy.wait_send()
        sent(tokens.at[:, 0, :, halves], in_send.at[0])

    ld_arrival.wait_recv()
    for half in range(2):
        decay_rows[:, half * ROWS : (half + 1) * ROWS] = ld_all[half].astype(F32)
    run = dot(decay_rows[...].astype(BF16), lower[...], ((1,), (1,)))
    run_rows[...] = run
    fade_rows[...] = jnp.exp(run[:, SPAN - 1 : SPAN] - run)
    end_rows[...] = jnp.broadcast_to(run[:, SPAN - 1 : SPAN], end_rows.shape)
    gain_own.wait()

    @pl.loop(0, nz)
    def _(t):
        b = order(t)
        first = 4 * b + 2 * core
        at = lax.broadcasted_iota(jnp.int32, (8, HD), 0)
        tile = jnp.where(at == 0, end_rows[pl.ds(first, 1), :], end_rows[pl.ds(first + 1, 1), :])
        z_send[b] = jnp.where(at < 2, tile, jnp.where(at == 2, gain[0:1, :], gain[1:2, :]))

        @pl.when(t < nz - 1)
        def _():
            facts_copy(b, z).start()

    z_recv[z] = z_send[z]
    for a in range(2):
        own_copy(a).wait()

    def send_part(u, part):
        @pl.loop(0, nz - 1)
        def _(t):
            over_z(l_send, l_recv, l_ss, l_rs, u, part, order(t), z).start()

    for u in range(2):
        @pl.loop(0, nz)
        def _(t):
            b = order(t)
            if u == 0:
                arrived(tokens.at[pl.ds(0, 2), other, :, columns(b, core)], in_recv.at[b])
            which = pl.ds(4 * b + 2 * core + u, 1)
            scaled = rows_of(0, b, u).T.astype(F32) * fade_rows[which, :]
            high = scaled.astype(BF16)
            low = (scaled - high.astype(F32)).astype(BF16)
            both = dot(jnp.concatenate([high, low], axis=0), rows_of(1, b, u))
            state = (both[:HD] + both[HD:]).astype(BF16)
            l_send[u, b] = state

            if u == 0:
                @pl.when(t < nz - 1)
                def _():
                    over_z(l_send, l_recv, l_ss, l_rs, u, 0, b, z).start()

        if u == 0:
            send_part(0, 1)
        l_recv[u, z] = l_send[u, z]

        if u == 1:
            arrived(z_recv.at[pl.ds(0, nz - 1)], z_sem.at[1])
            total = lax.fori_loop(0, nz, lambda b, sums: sums + z_recv[b], jnp.zeros((8, HD), F32))
            for v in range(2):
                d_send[v] = jnp.broadcast_to(total[v : v + 1], (PIECE, HD))

            @pl.loop(1, ns)
            def _(t):
                decay_copy(lax.rem(seq + t, ns), seq).start()

            d_recv[seq] = d_send[turn]

            @pl.loop(0, nz)
            def _(t):
                swap_copy(2, t).start()

    def l_done():
        sent(l_send.at[:, pl.ds(0, nz - 1)], l_ss.at[0])

    send_part(1, 0)

    own_copy(2).wait()
    arrived(tokens.at[2, other, :, halves], in_recv.at[nz])

    def inside(b):
        for u in range(2):
            which = pl.ds(4 * b + 2 * core + u, 1)
            token = jnp.broadcast_to(decay_rows[which, :], (HD, SPAN)).astype(BF16)
            run = dot(lower[...], token, ((1,), (1,)))
            run_all[2 * b + u] = run
            scores = dot(rows_of(2, b, u), rows_of(0, b, u), ((1,), (1,)))
            gap = jnp.concatenate([run, run], axis=1) - run_rows[which, :]
            here = (
                lax.broadcasted_iota(jnp.int32, (SPAN, SPAN), 0)
                >= lax.broadcasted_iota(jnp.int32, (SPAN, SPAN), 1)
            )
            weights = (scores * jnp.exp(jnp.where(here, gap, NEVER))).astype(BF16)
            within[2 * b + u] = dot(weights, rows_of(1, b, u))


    def column_sum(u, part):
        arrived(l_recv.at[u, pl.ds(0, nz - 1), part_rows[part]], l_rs.at[2 * u + part])

        def add(b, sums):
            return jnp.exp(z_recv[b, u : u + 1, :]) * sums + l_recv[u, b, part_rows[part], :].astype(F32)

        state = lax.fori_loop(0, nz, add, jnp.zeros((HALF, HD), F32), unroll=True)
        for g in range(near_ns):
            x_send[2 * (near_ns * part + g) + u] = state[PIECE * g : PIECE * (g + 1)]

        @pl.loop(0, near_ns, unroll=True)
        def _(t):
            g = near_ns * part + lax.rem(group + 1 + t, near_ns)

            @pl.when(2 * g + u != seq)
            def _():
                sum_copy(u, g, seq).start()

        @pl.when((turn == u) & (lax.div(group, near_ns) == part))
        def _():
            x_recv[seq] = x_send[seq]

    def columns_scan(u, part):
        @pl.when((turn == u) & (lax.div(group, near_ns) == part))
        def _():
            arrived(x_recv.at[pl.ds(0, ns - 1)], x_sem.at[1])
            piece = cached[...]
            for i in range(ns):
                e_send[i] = piece
                piece = jnp.exp(d_recv[i]) * piece + x_recv[i]
            fin_all[u] = piece

            @pl.loop(0, ns - 1, unroll=True)
            def _(t):
                far = lax.rem(seq + 1 + lax.rem(t + 3 * ns // 8 - 1, ns - 1), ns)
                entry_copy(u, group, far).start()

            e_recv[u, piece_rows(group), :] = e_send[seq]

    def give(u, part):
        landed = e_sem.at[1 + 2 * u + part]
        owner = (turn == u) & (lax.div(group, near_ns) == part)

        @pl.when(owner)
        def _():
            arrived(e_recv.at[u, pl.ds(0, HALF - PIECE)], landed)

        @pl.when(jnp.logical_not(owner))
        def _():
            arrived(e_recv.at[u, pl.ds(0, HALF)], landed)

        def step(b, state):
            s_send[u, b, part_rows[part], :] = state.astype(BF16)

            @pl.when(b != z)
            def _():
                over_z(s_send, s_recv, s_ss, s_rs, u, part, b, z, True).start()

            return jnp.exp(z_recv[b, u : u + 1, :]) * state + l_recv[u, b, part_rows[part], :].astype(F32)

        lax.fori_loop(0, nz, step, e_recv[u, HALF * part : HALF * (part + 1), :], unroll=True)

        if part == 1:
            s_recv[u, z] = s_send[u, z]

    column_sum(0, 0)
    send_part(1, 1)
    pl.loop(0 * nz // 8, 2 * nz // 8)(inside)
    column_sum(0, 1)
    pl.loop(2 * nz // 8, 4 * nz // 8)(inside)
    column_sum(1, 0)
    cached_own.wait()
    arrived(d_recv.at[pl.ds(0, ns - 1)], d_sem.at[1])
    columns_scan(0, 0)
    column_sum(1, 1)
    columns_scan(0, 1)
    pl.loop(4 * nz // 8, 8 * nz // 8)(inside)
    give(0, 0)
    columns_scan(1, 0)
    give(0, 1)
    columns_scan(1, 1)
    give(1, 0)
    swaps_done()
    l_done()
    give(1, 1)

    def scan_done():
        sent(x_send.at[pl.ds(0, ns - 1)], x_sem.at[0])
        sent(e_send.at[pl.ds(0, ns - 1)], e_sem.at[0])
        sent(d_recv.at[pl.ds(0, ns - 1)], d_sem.at[0])
        sent(z_send.at[pl.ds(0, nz - 1)], z_sem.at[0])

    def s_done():
        sent(s_send.at[:, pl.ds(0, nz - 1)], s_ss.at[0])

    def fin_copy(slot):
        return pltpu.make_async_remote_copy(
            fin_all.at[slot], fin_all.at[slot], f_sem.at[0], f_sem.at[1],
            device_id=(2 * group + 1 - turn, head), device_id_type=MESH,
        )

    fin_copy(turn).start()

    mine_rows = pl.ds(pl.multiple_of(core * ROWS, ROWS), ROWS)
    other_rows = pl.ds(pl.multiple_of(other * ROWS, ROWS), ROWS)

    def out_own(b):
        return pltpu.make_async_copy(out.at[b, mine_rows], att_ref.at[:, columns(b, core)], o_sem.at[0])

    def out_swap(b):
        return to_partner(out.at[b, other_rows], att_ref.at[:, columns(b, core)], o_sem.at[1], o_sem.at[2])

    def output(u):
        for part in range(2 - u):
            arrived(s_recv.at[u, pl.ds(0, nz - 1), part_rows[part]], s_rs.at[2 * u + part])

        @pl.loop(0, nz)
        def _(t):
            b = near(t)

            if u == 1:
                @pl.when(t > 0)
                def _():
                    arrived(s_recv.at[u, b, part_rows[1]], s_rs.at[3 + b])

            carried = dot(rows_of(2, b, u), s_recv[u, b])
            mixed = within[2 * b + u] + carried * jnp.exp(run_all[2 * b + u])
            mean = jnp.mean(mixed * mixed, axis=1, keepdims=True)
            normed = mixed * lax.rsqrt(mean + 1e-6) * z_recv[b, 2 + u : 3 + u, :]
            out[b, :, u * HD : (u + 1) * HD] = normed.astype(BF16)
            if u == 1:
                out_own(b).start()
                out_swap(b).start()

    output(0)
    scan_done()
    output(1)
    fin_copy(1 - turn).wait_recv()
    for u in range(2):
        fin_ref[u] = jnp.where(turn == 0, fin_all[u, 0:4, :], fin_all[u, 4:8, :])

    fin_copy(turn).wait_send()
    s_done()

    some = out.at[:, pl.ds(0, ROWS)]
    pltpu.make_async_copy(some, some, o_sem.at[0]).wait()
    sent(some, o_sem.at[1])
    arrived(some, o_sem.at[2])


def local(ns, nz, queries, keys, values, log_decay, cached_state, norm_gain):
    anywhere = pl.BlockSpec(memory_space=pl.ANY)
    vmem = pl.BlockSpec(memory_space=pltpu.VMEM)
    dma = pltpu.SemaphoreType.DMA
    heads = log_decay.shape[1]
    return pl.pallas_call(
        functools.partial(kernel, ns, nz),
        out_shape=(
            pltpu.VMEM(queries.shape, BF16),
            pltpu.VMEM((2, HD // ns, HD), F32),
        ),
        in_specs=[anywhere] * 6,
        out_specs=(anywhere, vmem),
        scratch_shapes=[
            pltpu.VMEM((3, 2) + queries.shape, BF16),
            pltpu.VMEM((2, heads, ROWS), BF16),
            pltpu.VMEM((heads, SPAN), F32),
            pltpu.VMEM((heads, SPAN), F32),
            pltpu.VMEM((heads, SPAN), F32),
            pltpu.VMEM((heads, HD), F32),
            pltpu.VMEM((SPAN, SPAN), BF16),
            pltpu.VMEM((2 * nz, SPAN, HD), F32),
            pltpu.VMEM((2 * nz, SPAN, HD), F32),
            pltpu.VMEM((2, nz, HD, HD), BF16),
            pltpu.VMEM((2, nz, HD, HD), BF16),
            pltpu.VMEM((ns, PIECE, HD), F32),
            pltpu.VMEM((ns, PIECE, HD), F32),
            pltpu.VMEM((ns, PIECE, HD), F32),
            pltpu.VMEM((2, HD, HD), F32),
            pltpu.VMEM((2, nz, HD, HD), BF16),
            pltpu.VMEM((2, nz, HD, HD), BF16),
            pltpu.VMEM((nz, SPAN, PAIR), BF16),
            pltpu.VMEM((2, PIECE, HD), F32),
            pltpu.VMEM((PIECE, HD), F32),
            pltpu.VMEM((2, HD), F32),
            pltpu.VMEM((nz, 8, HD), F32),
            pltpu.VMEM((nz, 8, HD), F32),
            pltpu.VMEM((2, PIECE, HD), F32),
            pltpu.VMEM((ns, PIECE, HD), F32),
            dma((3,)), dma((1,)), dma((nz + 1,)), dma((2,)),
            dma((1,)), dma((4,)), dma((2,)), dma((5,)), dma((1,)), dma((3 + nz,)),
            dma((3,)), dma((2,)), dma((3,)), dma((2,)), dma((2,)),
        ],
        compiler_params=pltpu.CompilerParams(
            collective_id=0, has_side_effects=True, vmem_limit_bytes=58 * 1024 * 1024
        ),
        cost_estimate=pl.CostEstimate(flops=10**9, bytes_accessed=8 * 2**20, transcendentals=2 * 10**6),
    )(queries, keys, values, log_decay.T, cached_state, norm_gain)


def solution(mesh):
    rows = P(("seq", "head"), None)
    return jax.shard_map(
        functools.partial(local, mesh.shape["seq"], mesh.shape["head"] // 2),
        mesh=mesh,
        in_specs=(rows, rows, rows, rows, P("head", None, None), P("head", None)),
        out_specs=(rows, P("head", "seq", None)),
        check_vma=False,
    )
```
